256 devices in a mesh: dp: 32 (over z_hi, y, core), pipe: 8 (over x, z_lo).
Axes of the slice: x: 4, y: 4, z: 8 (z_hi: 4, z_lo: 2; z = z_hi * 2 + z_lo), core: 2. Of those that a mesh axis runs over, the one named last changes fastest.
Arguments:
- hidden: bfloat16 [8, 64, 64, 1792], P('pipe', 'dp'), may hold values from -6 to 6
- selective_head_input: bfloat16 [8, 64, 64, 3584], P('pipe', 'dp'), may hold values from -6 to 6
- selective_output_gradient: bfloat16 [8, 64, 64, 3584], P('pipe', 'dp'), may hold values from -6 to 6
- final_output_gradient: bfloat16 [64, 64, 1792], P('dp'), may hold values from -6 to 6
- shared_projection_weight: bfloat16 [1792, 1792], replicated, may hold values from -0.125 to 0.125
- shared_norm_gain: float32 [1792], replicated, may hold values from 0.5 to 1.5
- adapter_down_weight: bfloat16 [8, 1792, 128], P('pipe'), may hold values from -0.125 to 0.125
- adapter_up_weight: bfloat16 [8, 128, 1792], P('pipe'), may hold values from -0.5 to 0.5
- selective_norm_gain: float32 [8, 1792], P('pipe'), may hold values from 0.5 to 1.5
- selective_coefficient_projection: bfloat16 [8, 1792, 184], P('pipe'), may hold values from -0.125 to 0.125
- step_size_bias: float32 [8, 56], P('pipe'), may hold values from -4 to -1
- decay: float32 [8, 56], P('pipe'), may hold values from 0.02 to 2
Outputs:
- section_grads: bfloat16 [8, 64, 64, 1792], P('pipe', 'dp')
- shared_weight_grad: float32 [1792, 1792], P('dp')
- shared_gain_grad: float32 [1792], P('dp')
- lora_down_grad: bfloat16 [8, 1792, 128], P('pipe')
- lora_up_grad: bfloat16 [8, 128, 1792], P('pipe')
- proj_grad: float32 [8, 1792, 184], P('pipe', 'dp')
- mamba_gain_grad: float32 [8, 1792], P('pipe', 'dp')
- dt_bias_grad: float32 [8, 56], P('pipe')
- decay_grad: float32 [8, 56], P('pipe')
The draws below stay inside these ranges and needn't reach their ends.
All inputs are finite; a program needn't handle non-finite values.
Results may differ from the reference program's by a relative error of at most 0.04.
Values may be sent and summed in bfloat16 or wider, within the bound.
No kernel may reach another device: no remote copies, remote signals or barrier semaphores. Data moves between devices by JAX's collectives and lax.ppermute only.
A program may use at most 128 MiB of HBM per device.

```python
import math
import jax
import jax.numpy as jnp
from jax import lax

HALF_FEATURES = 1792
HEADS = 56
ADAPTER_RANK = 128
TOK = 64
SECTION_COUNT = 8
BATCH = 64
INNER = 3584
PROJ = 184


def shard_levels(stream_key, extent, shards, smallest, high):
    factor_of, own = 1.0, jax.random.fold_in(stream_key, 6)
    for dim, parts in shards:
        heights = jnp.exp(jax.random.uniform(jax.random.fold_in(own, dim), (parts,), jnp.float32, smallest / len(shards), high / len(shards)))
        factor_of = factor_of * jnp.repeat(heights, extent[dim] // parts).reshape([-1 if axis == dim else 1 for axis in range(len(extent))])
    return factor_of


def noise(key, dims, width, reach, pieces=(), dtype=jnp.bfloat16):
    entries = jax.random.normal(key, dims, jnp.float32) * width
    if len(pieces) > 0:
        entries = shard_levels(key, dims, pieces, -0.22, 0.18) * entries
    return jnp.clip(entries, min=-reach, max=reach).astype(dtype)


def setup_inputs(seed: int = 0) -> dict:
    streams_of = jax.random.split(jax.random.key(seed), 13)
    return {
        "hidden": noise(streams_of[0], (SECTION_COUNT, BATCH, TOK, HALF_FEATURES), 1.0, 6.0, ((0, 8), (1, 32))),
        "selective_head_input": noise(streams_of[1], (SECTION_COUNT, BATCH, TOK, INNER), 1.0, 6.0, ((0, 8), (1, 32))),
        "selective_output_gradient": noise(streams_of[2], (SECTION_COUNT, BATCH, TOK, INNER), 1.0, 6.0, ((0, 8), (1, 32))),
        "final_output_gradient": noise(streams_of[3], (BATCH, TOK, HALF_FEATURES), 1.0, 6.0, ((0, 32),)),
        "shared_projection_weight": noise(streams_of[4], (HALF_FEATURES, HALF_FEATURES), HALF_FEATURES ** -0.5, 0.125),
        "shared_norm_gain": jnp.clip(1.0 + 0.1 * jax.random.normal(streams_of[5], (HALF_FEATURES,), jnp.float32), 0.5, 1.5),
        "adapter_down_weight": noise(streams_of[6], (SECTION_COUNT, HALF_FEATURES, ADAPTER_RANK), HALF_FEATURES ** -0.5, 0.125, ((0, 8),)),
        "adapter_up_weight": noise(streams_of[7], (SECTION_COUNT, ADAPTER_RANK, HALF_FEATURES), ADAPTER_RANK ** -0.5, 0.5, ((0, 8),)),
        "selective_norm_gain": jnp.clip(1.0 + 0.1 * jax.random.normal(streams_of[8], (SECTION_COUNT, HALF_FEATURES), jnp.float32), 0.5, 1.5),
        "selective_coefficient_projection": noise(streams_of[9], (SECTION_COUNT, HALF_FEATURES, PROJ), HALF_FEATURES ** -0.5, 0.125, ((0, 8),)),
        "step_size_bias": jnp.clip(-4.0 + 3.0 * jax.random.uniform(streams_of[10], (SECTION_COUNT, HEADS), jnp.float32) ** shard_levels(streams_of[10], (SECTION_COUNT, HEADS), ((0, 8),), -0.2, 0.2), -4.0, -1.0),
        "decay": jnp.clip(jnp.exp(math.log(2.0) - 4.6051702 * jax.random.uniform(streams_of[11], (SECTION_COUNT, HEADS), jnp.float32) ** shard_levels(streams_of[11], (SECTION_COUNT, HEADS), ((0, 8),), -0.2, 0.2)), 0.02, 2.0),
    }


epsilon = 1e-05

def rms_factor(values):
    return lax.rsqrt(lax.optimization_barrier(jnp.mean(values * values, axis=-1, keepdims=True)) + epsilon)

def ssd_mix(projected, bias_step, decay_rate, head_input):
    heads_count = bias_step.shape[0]
    state_size = (projected.shape[1] - heads_count) // 2
    length = head_input.shape[0]
    b_coef = projected[:, :state_size]
    c_coef = projected[:, state_size:2 * state_size]
    step_size = jax.nn.softplus(projected[:, 2 * state_size:] + bias_step)
    running = jnp.cumsum(step_size, axis=0)
    positions = jnp.arange(length)
    causal = (positions[:, None] >= positions[None, :])[:, :, None]
    spread = jnp.where(causal, running[:, None, :] - running[None, :, :], 0.0)
    kernel = jnp.where(causal, jnp.exp(-decay_rate * spread), 0.0)
    intersection = jnp.dot(c_coef, b_coef.T, precision=lax.Precision.HIGHEST)
    weights = kernel * intersection[:, :, None] * step_size[None, :, :]
    values = head_input.astype(jnp.float32).reshape(length, heads_count, -1)
    mixed = jnp.einsum('ijh,jhp->ihp', weights, values, precision=lax.Precision.HIGHEST)
    return mixed.reshape(length, -1)

def section_back(hidden_seq, head_seq, head_cot, arriving, parameter_tuple):
    shared_matrix, shared_g, down_adapter_map, up_adapter_map, mamba_g, proj_w, bias_step, decay_rate = parameter_tuple
    stream = hidden_seq.astype(jnp.float32)
    scale_zero = rms_factor(stream)
    base = stream * scale_zero
    normalized_input = (base * shared_g).astype(jnp.bfloat16)
    adapter_middle_value = jnp.dot(normalized_input, down_adapter_map, preferred_element_type=jnp.float32).astype(jnp.bfloat16)
    activation = jnp.dot(normalized_input, shared_matrix, preferred_element_type=jnp.float32) + jnp.dot(adapter_middle_value, up_adapter_map, preferred_element_type=jnp.float32)
    gate_sig = jax.nn.sigmoid(activation)
    middle = stream + activation * gate_sig
    scale_one = rms_factor(middle)
    inner = middle * scale_one
    selective_layer_input = (inner * mamba_g).astype(jnp.bfloat16)
    projected = jnp.dot(selective_layer_input, proj_w, preferred_element_type=jnp.float32)
    _, pullback = jax.vjp(lambda proj_arg, bias_arg, decay_arg: ssd_mix(proj_arg, bias_arg, decay_arg, head_seq), projected, bias_step, decay_rate)
    projection_cotangent, bias_cot, decay_cot = pullback(head_cot.astype(jnp.float32))
    projection_cotangent = projection_cotangent.astype(jnp.bfloat16)
    mamba_cot = jnp.dot(projection_cotangent, proj_w.T, preferred_element_type=jnp.float32)
    gain_part = lax.optimization_barrier(jnp.sum(mamba_cot * inner, axis=0))
    weighted = mamba_cot * mamba_g
    stream_cot = arriving.astype(jnp.float32) + scale_one * (weighted - inner * lax.optimization_barrier(jnp.mean(weighted * inner, axis=-1, keepdims=True)))
    activation_cotangent = (stream_cot * gate_sig * (1.0 + activation * (1.0 - gate_sig))).astype(jnp.bfloat16)
    middle_cotangent = jnp.dot(activation_cotangent, up_adapter_map.T, preferred_element_type=jnp.float32).astype(jnp.bfloat16)
    normed_cot = jnp.dot(activation_cotangent, shared_matrix.T, preferred_element_type=jnp.float32) + jnp.dot(middle_cotangent, down_adapter_map.T, preferred_element_type=jnp.float32)
    shared_part = lax.optimization_barrier(jnp.sum(normed_cot * base, axis=0))
    pulled = normed_cot * shared_g
    previous = stream_cot + scale_zero * (pulled - base * lax.optimization_barrier(jnp.mean(pulled * base, axis=-1, keepdims=True)))
    saved_activations = (normalized_input, adapter_middle_value, activation_cotangent, middle_cotangent, selective_layer_input, projection_cotangent)
    partials = (shared_part, gain_part, bias_cot, decay_cot)
    return (previous.astype(jnp.bfloat16), saved_activations, partials)

def flatten_rows(array):
    return array.reshape(-1, array.shape[-1])

def reference(hidden, selective_head_input, selective_output_gradient, final_output_gradient, shared_projection_weight, shared_norm_gain, adapter_down_weight, adapter_up_weight, selective_norm_gain, selective_coefficient_projection, step_size_bias, decay):
    incoming = final_output_gradient
    grad_list = [None] * SECTION_COUNT
    down_list = [None] * SECTION_COUNT
    up_adapter_list = [None] * SECTION_COUNT
    proj_list = [None] * SECTION_COUNT
    gain_list = [None] * SECTION_COUNT
    bias_list = [None] * SECTION_COUNT
    decay_list = [None] * SECTION_COUNT
    shared_total = jnp.zeros((HALF_FEATURES, HALF_FEATURES), jnp.float32)
    shared_gain_total = jnp.zeros((HALF_FEATURES,), jnp.float32)
    for section_number in range(SECTION_COUNT - 1, -1, -1):
        parameter_tuple = (shared_projection_weight, shared_norm_gain, adapter_down_weight[section_number], adapter_up_weight[section_number], selective_norm_gain[section_number], selective_coefficient_projection[section_number], step_size_bias[section_number], decay[section_number])
        results = lax.map(lambda items: section_back(items[0], items[1], items[2], items[3], parameter_tuple), (hidden[section_number], selective_head_input[section_number], selective_output_gradient[section_number], incoming))
        previous, saved_activations, partials = results
        normalized_input, adapter_middle_value, activation_cotangent, middle_cotangent, selective_layer_input, projection_cotangent = saved_activations
        shared_part, gain_part, bias_cot, decay_cot = partials
        shared_total = shared_total + jnp.dot(flatten_rows(normalized_input).T, flatten_rows(activation_cotangent), preferred_element_type=jnp.float32)
        shared_gain_total = shared_gain_total + lax.optimization_barrier(jnp.sum(shared_part, axis=0))
        down_list[section_number] = jnp.dot(flatten_rows(normalized_input).T, flatten_rows(middle_cotangent), preferred_element_type=jnp.float32).astype(jnp.bfloat16)
        up_adapter_list[section_number] = jnp.dot(flatten_rows(adapter_middle_value).T, flatten_rows(activation_cotangent), preferred_element_type=jnp.float32).astype(jnp.bfloat16)
        proj_list[section_number] = jnp.dot(flatten_rows(selective_layer_input).T, flatten_rows(projection_cotangent), preferred_element_type=jnp.float32)
        gain_list[section_number] = lax.optimization_barrier(jnp.sum(gain_part, axis=0))
        bias_list[section_number] = lax.optimization_barrier(jnp.sum(bias_cot, axis=0))
        decay_list[section_number] = lax.optimization_barrier(jnp.sum(decay_cot, axis=0))
        grad_list[section_number] = previous
        incoming = previous
    return (jnp.stack(grad_list), shared_total, shared_gain_total, jnp.stack(down_list), jnp.stack(up_adapter_list), jnp.stack(proj_list), jnp.stack(gain_list), jnp.stack(bias_list), jnp.stack(decay_list))
```

```python
import jax
import jax.numpy as jnp
import numpy as np
from jax import lax
from jax.experimental import pallas as pl
from jax.experimental.pallas import tpu as pltpu
from jax.sharding import Mesh, PartitionSpec as P

EPS = 1e-05
F32 = jnp.float32
BF16 = jnp.bfloat16
HIGHEST = lax.Precision.HIGHEST

WIDTH = 1792
INNER = 3584
RANK = 128
HEADS = 56
TOK = 64
ROWS = 128
CHUNK = 256
CHUNKS = INNER // CHUNK
SLICE = 224

DP = ("z_hi", "y", "core")
PIPE = ("x", "z_lo")


def nn(a, b):
    return jnp.dot(a, b, preferred_element_type=F32)


def nt(a, b):
    return lax.dot_general(a, b, (((1,), (1,)), ((), ())), preferred_element_type=F32)


def exact(a, b):
    return jnp.dot(a, b, preferred_element_type=F32, precision=HIGHEST)


def two_parts(value):
    high = value.astype(BF16)
    low = (value - high.astype(F32)).astype(BF16)
    return high, low


def lanes_and_rows(shape):
    return lax.broadcasted_iota(jnp.int32, shape, 1), lax.broadcasted_iota(jnp.int32, shape, 0)


def ssd_back(bc, raw, decay_row, expand, gather, head_ref, cot_ref, expanded, stack):
    lane128, _ = lanes_and_rows((TOK, 128))
    low_half = lane128 < TOK
    lane64, row64 = lanes_and_rows((TOK, TOK))
    lower = (row64 >= lane64).astype(F32)
    upper = (row64 <= lane64).astype(F32)
    steps, parts = [], []
    for n in range(2):
        step = jax.nn.softplus(raw[n * TOK : (n + 1) * TOK])
        step = jnp.where(lane128 < HEADS, step, 0.0)
        running = exact(lower, step)
        steps.append(step)
        for value in (running, step):
            first = value.astype(BF16).astype(F32)
            rest = value - first
            second = rest.astype(BF16).astype(F32)
            third = rest - second
            left = jnp.where(low_half, first, pltpu.roll(second, TOK, 1))
            parts.append(jnp.concatenate([left, third], axis=1).astype(BF16))
    expanded[...] = nn(jnp.concatenate(parts, axis=0), expand[...])
    decay_wide = jnp.broadcast_to(decay_row, (8, 128))
    d_first = decay_wide.astype(BF16).astype(F32)
    d_rest = decay_wide - d_first
    d_second = d_rest.astype(BF16).astype(F32)
    lane8, _ = lanes_and_rows((8, 128))
    d_left = jnp.where(lane8 < TOK, d_first, pltpu.roll(d_second, TOK, 1))
    d_parts = jnp.concatenate([d_left, d_rest - d_second], axis=1).astype(BF16)
    decay_lanes = nn(d_parts, expand[...])[0:1]

    lane_c, row_c = lanes_and_rows((TOK, CHUNK))
    token_c = lane_c % TOK
    causal = row_c >= token_c
    diagonal = row_c == token_c
    lane_b, row_b = lanes_and_rows((CHUNK, CHUNK))
    block = (lane_b // TOK) == (row_b // TOK)
    row16 = lax.broadcasted_iota(jnp.int32, (16, CHUNK), 0)
    d_bc = []
    for n in range(2):
        rows = slice(n * TOK, (n + 1) * TOK)
        here = bc[rows]
        rolled = pltpu.roll(here, TOK, 1)
        b_only = jnp.where(low_half, here, 0.0)
        crossing = lax.dot_general(
            rolled,
            jnp.concatenate([b_only] * 4, axis=0),
            (((1,), (1,)), ((), ())),
            preferred_element_type=F32,
            precision=HIGHEST,
        )
        d_cross = jnp.zeros((TOK, CHUNK), F32)
        for g in range(CHUNKS):
            cols = slice(g * CHUNK, (g + 1) * CHUNK)
            heads = jnp.concatenate([head_ref[rows, cols]] * 4, axis=0)
            heads = jnp.where(block, heads, jnp.zeros_like(heads))
            grad = nt(cot_ref[rows, cols], heads)
            run = expanded[n * ROWS : n * ROWS + TOK, cols]
            step = expanded[n * ROWS + TOK : (n + 1) * ROWS, cols]
            run_j = jnp.sum(jnp.where(diagonal, run, 0.0), axis=0, keepdims=True)
            step_j = jnp.sum(jnp.where(diagonal, step, 0.0), axis=0, keepdims=True)
            spread = jnp.where(causal, run - run_j, 0.0)
            kernel = jnp.where(causal, jnp.exp(-decay_lanes[:, cols] * spread), 0.0)
            scored = grad * kernel
            d_cross = d_cross + scored * step_j
            per_step = scored * crossing
            col = jnp.sum(per_step, axis=0, keepdims=True)
            mass = per_step * step_j
            balance = mass - jnp.where(diagonal, col * step_j, 0.0)
            direct = jnp.where(diagonal, col, 0.0)
            spent = jnp.sum(mass * spread, axis=0, keepdims=True)
            base_row = n * 272
            high, low = two_parts(balance)
            stack[base_row : base_row + 64, cols] = high
            stack[base_row + 64 : base_row + 128, cols] = low
            high, low = two_parts(direct)
            stack[base_row + 128 : base_row + 192, cols] = high
            stack[base_row + 192 : base_row + 256, cols] = low
            high = spent.astype(BF16).astype(F32)
            tail = jnp.where(row16 == 0, high, jnp.where(row16 == 1, spent - high, 0.0))
            stack[base_row + 256 : base_row + 272, cols] = tail.astype(BF16)
        d_cross = d_cross[:, :128] + d_cross[:, 128:]
        d_cross = (d_cross + pltpu.roll(d_cross, TOK, 1))[:, :TOK]
        c_low = jnp.where(low_half, rolled, 0.0)
        b_high = jnp.where(low_half, 0.0, rolled)
        d_bc.append(exact(d_cross.T, c_low) + exact(d_cross, b_high))
    gathered = nn(stack[...], gather[...])
    d_raw, decay_cot = [], jnp.zeros((1, 128), F32)
    for n in range(2):
        at = n * 272
        balance = gathered[at : at + 64] + gathered[at + 64 : at + 128]
        direct = gathered[at + 128 : at + 192] + gathered[at + 192 : at + 256]
        spent = jnp.sum(gathered[at + 256 : at + 272], axis=0, keepdims=True)
        d_step = direct + exact(upper, -decay_row * balance)
        d_raw.append(d_step * jax.nn.sigmoid(raw[n * TOK : (n + 1) * TOK]))
        decay_cot = decay_cot - spent
    return jnp.concatenate(d_bc, axis=0), jnp.concatenate(d_raw, axis=0), decay_cot


def front_kernel(
    hidden_ref, head_ref, cot_ref, w_ref, down_ref, up_ref, bc_w_ref, step_w_ref, g_ref, mg_ref, bias_ref, decay_ref,
    expand_ref, gather_ref,
    const_ref, slope_ref, base_ref, scale_ref, normed_t_ref, mid_ref, proj_ref, small_ref,
    expanded, stack,
):
    stream = hidden_ref[...].astype(F32)
    scale0 = lax.rsqrt(jnp.mean(stream * stream, axis=1, keepdims=True) + EPS)
    base = stream * scale0
    normed = (base * g_ref[...]).astype(BF16)
    base_ref[...] = base
    scale_ref[...] = jnp.broadcast_to(scale0, (ROWS, 128))
    normed_t_ref[...] = normed.T
    mid = nn(normed, down_ref[...]).astype(BF16)
    mid_ref[...] = mid
    act = nn(normed, w_ref[...]) + nn(mid, up_ref[...])
    gate = jax.nn.sigmoid(act)
    slope_ref[...] = gate * (1.0 + act * (1.0 - gate))
    middle = stream + act * gate
    scale1 = lax.rsqrt(jnp.mean(middle * middle, axis=1, keepdims=True) + EPS)
    inner = middle * scale1
    gain = mg_ref[...]
    mamba_in = (inner * gain).astype(BF16)
    bc = nn(mamba_in, bc_w_ref[...])
    raw = nn(mamba_in, step_w_ref[...]) + bias_ref[...]
    d_bc, d_raw, decay_cot = ssd_back(
        bc, raw, decay_ref[...], expand_ref, gather_ref, head_ref, cot_ref, expanded, stack
    )
    d_bc, d_raw16 = d_bc.astype(BF16), d_raw.astype(BF16)
    mamba_cot = nt(d_bc, bc_w_ref[...]) + nt(d_raw16, step_w_ref[...])
    pulled = mamba_cot * inner
    weighted = mamba_cot * gain
    const_ref[...] = scale1 * (weighted - inner * jnp.mean(pulled * gain, axis=1, keepdims=True))
    lane, _ = lanes_and_rows((ROWS, 256))
    ones = jnp.where(lane == 184, 1.0, 0.0).astype(BF16)
    proj_ref[...] = (
        nn(mamba_in.T, jnp.concatenate([d_bc, d_raw16], axis=1)) + nn(pulled.astype(BF16).T, ones)
    ).astype(BF16)
    _, row8 = lanes_and_rows((8, 128))
    bias_cot = jnp.sum(d_raw, axis=0, keepdims=True)
    small_ref[...] = jnp.where(row8 == 0, bias_cot, jnp.where(row8 == 1, decay_cot, 0.0))


def stage_math(arriving, const, slope, base, scale0, w_ref, down_ref, up_ref, g_ref):
    stream_cot = arriving + const
    act_cot = (stream_cot * slope).astype(BF16)
    mid_cot = nt(act_cot, up_ref[...]).astype(BF16)
    normed_cot = nt(act_cot, w_ref[...]) + nt(mid_cot, down_ref[...])
    pulled = normed_cot * g_ref[...]
    previous = stream_cot + scale0 * (pulled - base * jnp.mean(pulled * base, axis=1, keepdims=True))
    return previous.astype(BF16), act_cot, mid_cot, normed_cot


def stage_kernel(
    arriving_ref, total_ref, const_ref, slope_ref, base_ref, scale_ref, w_ref, down_ref, up_ref, g_ref,
    previous_ref, sum_ref,
):
    arriving = arriving_ref[...].astype(F32)
    sum_ref[...] = (total_ref[...].astype(F32) + arriving).astype(BF16)
    previous_ref[...] = stage_math(
        arriving, const_ref[...], slope_ref[...], base_ref[...], scale_ref[:, 0:1], w_ref, down_ref, up_ref, g_ref
    )[0]


def last_kernel(
    arriving0_ref, total0_ref, arriving1_ref, total1_ref, const_ref, slope_ref, base_ref, scale_ref,
    w_ref, down_ref, up_ref, g_ref, normed_t_ref, mid_ref,
    previous_ref, act_ref, lora_down_ref, lora_up_ref, shared_gain_ref,
):
    arriving = jnp.concatenate(
        [
            arriving0_ref[...].astype(F32) + total0_ref[...].astype(F32),
            arriving1_ref[...].astype(F32) + total1_ref[...].astype(F32),
        ],
        axis=0,
    )
    base = base_ref[...]
    previous, act_cot, mid_cot, normed_cot = stage_math(
        arriving, const_ref[...], slope_ref[...], base, scale_ref[:, 0:1], w_ref, down_ref, up_ref, g_ref
    )
    previous_ref[...] = previous
    padded = jnp.concatenate([act_cot, jnp.zeros((ROWS, 128), BF16)], axis=1)
    for q in range(8):
        act_ref[q] = padded[:, q * SLICE : q * SLICE + 256]
    lora_down_ref[...] = nn(normed_t_ref[...], mid_cot).astype(BF16)
    lora_up_ref[...] = nn(mid_ref[...].T, act_cot).astype(BF16)
    shared_gain_ref[...] = jnp.sum(normed_cot * base, axis=0, keepdims=True)


def shape(dims, dtype):
    return jax.ShapeDtypeStruct(dims, dtype)


def params(megabytes):
    return pltpu.CompilerParams(vmem_limit_bytes=megabytes * 1024 * 1024)


def one_hots():
    rows = np.arange(256)[:, None]
    lanes = np.arange(INNER)[None, :]
    expand = ((rows < 192) & (rows % TOK == lanes // TOK)).astype(np.float32)
    gather = (np.arange(INNER)[:, None] // TOK == np.arange(128)[None, :]).astype(np.float32)
    return jnp.asarray(expand, BF16), jnp.asarray(gather, BF16)


def front(hidden, heads, cots, w, down, up, bc_w, step_w, g, mg, bias, decay):
    expand, gather = one_hots()
    return pl.pallas_call(
        front_kernel,
        out_shape=(
            shape((ROWS, WIDTH), F32),
            shape((ROWS, WIDTH), F32),
            shape((ROWS, WIDTH), F32),
            shape((ROWS, 128), F32),
            shape((WIDTH, ROWS), BF16),
            shape((ROWS, RANK), BF16),
            shape((WIDTH, 256), BF16),
            shape((8, 128), F32),
        ),
        scratch_shapes=[pltpu.VMEM((256, INNER), F32), pltpu.VMEM((544, INNER), BF16)],
        compiler_params=params(48),
        cost_estimate=pl.CostEstimate(flops=3_000_000_000, bytes_accessed=14_000_000, transcendentals=1_000_000),
    )(hidden, heads, cots, w, down, up, bc_w, step_w, g, mg, bias, decay, expand, gather)


def stage(arriving, total, const, slope, base, scale, w, down, up, g):
    return pl.pallas_call(
        stage_kernel,
        out_shape=(shape((TOK, WIDTH), BF16), shape((TOK, WIDTH), BF16)),
        compiler_params=params(24),
        cost_estimate=pl.CostEstimate(flops=500_000_000, bytes_accessed=9_000_000, transcendentals=0),
    )(arriving, total, const, slope, base, scale, w, down, up, g)


def last(arriving0, total0, arriving1, total1, const, slope, base, scale, w, down, up, g, normed_t, mid):
    return pl.pallas_call(
        last_kernel,
        out_shape=(
            shape((ROWS, WIDTH), BF16),
            shape((8, ROWS, 256), BF16),
            shape((WIDTH, RANK), BF16),
            shape((RANK, WIDTH), BF16),
            shape((1, WIDTH), F32),
        ),
        compiler_params=params(32),
        cost_estimate=pl.CostEstimate(flops=1_000_000_000, bytes_accessed=14_000_000, transcendentals=0),
    )(arriving0, total0, arriving1, total1, const, slope, base, scale, w, down, up, g, normed_t, mid)


def swap_cores(value):
    return lax.ppermute(value, "core", [(0, 1), (1, 0)])


def halves(value, core):
    own = lax.dynamic_index_in_dim(value, core, 1, keepdims=False)
    other = lax.dynamic_index_in_dim(value, 1 - core, 1, keepdims=False)
    return own, other


def summed(value, axis):
    return jnp.sum(value.astype(F32), axis=axis)


def local(hidden, heads, cots, final, w, g, down, up, mg, proj_w, bias, decay):
    core = lax.axis_index("core")
    place = lax.axis_index(PIPE)
    hidden, heads, cots = (a[0].reshape(ROWS, a.shape[-1]) for a in (hidden, heads, cots))
    down, up, proj_w = down[0], up[0], proj_w[0]
    bc_w, step_w = proj_w[:, :128], jnp.pad(proj_w[:, 128:], ((0, 0), (0, 128 - HEADS)))
    wide = lambda v: jnp.pad(v, ((0, 0), (0, 128 - HEADS)))
    g_row = g[None]
    const, slope, base, scale, normed_t, mid, proj_part, small = front(
        hidden, heads, cots, w, down, up, bc_w, step_w, g_row, mg, wide(bias), wide(decay)
    )

    own_t, other_t = halves(normed_t.reshape(16, 2, 56, ROWS), core)
    pair_t = jnp.concatenate([own_t, swap_cores(other_t)], axis=-1).reshape(896, 256)
    all_t = lax.all_gather(pair_t, PIPE, axis=0, tiled=False)

    first = jnp.where(place == 7, final, jnp.zeros_like(final))
    arriving = [first[0], first[1]]
    totals = [jnp.zeros((TOK, WIDTH), BF16)] * 2
    for tick in range(7):
        for n in range(2):
            rows = slice(n * TOK, (n + 1) * TOK)
            previous, totals[n] = stage(
                arriving[n], totals[n], const[rows], slope[rows], base[rows], scale[rows], w, down, up, g_row
            )
            arriving[n] = lax.ppermute(previous, PIPE, [(7 - tick, 6 - tick)])
    previous, act, lora_down, lora_up, shared_gain = last(
        arriving[0], totals[0], arriving[1], totals[1], const, slope, base, scale, w, down, up, g_row, normed_t, mid
    )

    proj_part = proj_part.reshape(32, 56, 256)
    lane = lax.broadcasted_iota(jnp.int32, (32, 56, 256), 2)
    heads_col = lambda v: v[:HEADS].astype(BF16)[None, :, None]
    gain_col = shared_gain.reshape(32, 56, 1).astype(BF16)
    proj_part = jnp.where(lane == 185, gain_col, proj_part)
    proj_part = jnp.where(lane == 186, heads_col(small[0]), proj_part)
    proj_part = jnp.where(lane == 187, heads_col(small[1]), proj_part)
    own_p, other_p = halves(proj_part.reshape(16, 2, 56, 256), core)
    tiles = lambda v: jnp.concatenate([v[:, :56], v[:, 56:]], axis=-1)
    down_tiles = tiles(lora_down.reshape(16, 112, 128))
    up_tiles = tiles(lora_up.reshape(16, 8, 14, 128).swapaxes(1, 2).reshape(16, 112, 128))
    own_l = jnp.where(core == 0, down_tiles, up_tiles)
    other_l = jnp.where(core == 0, up_tiles, down_tiles)
    swapped = swap_cores(jnp.concatenate([other_p, other_l], axis=-1))
    terms = (jnp.concatenate([own_p, own_l], axis=-1).astype(F32) + swapped.astype(F32)).astype(BF16)

    act_own = lax.all_to_all(act, PIPE, 0, 0, tiled=True)
    act_all = jnp.concatenate([act_own, swap_cores(act_own)], axis=1)
    shared = jnp.einsum("srk,skc->rc", all_t, act_all, preferred_element_type=F32)
    shared = shared.astype(BF16).reshape(16, 56, 256)
    terms = jnp.concatenate([shared, terms], axis=-1).reshape(4, 4, 56, 768)
    terms = summed(lax.all_to_all(terms, "y", 1, 1, tiled=True), 1).astype(BF16)
    terms = summed(lax.all_to_all(terms, "z_hi", 0, 0, tiled=True), 0)

    proj_grad = terms[:, 256:440]
    mamba_gain = terms[:, 440]
    bias_grad = terms[:, 442]
    decay_grad = terms[:, 443]
    lane = lax.broadcasted_iota(jnp.int32, (56, 256), 1)
    block = jnp.where(lane == SLICE, terms[:, 441:442], terms[:, :256]).astype(BF16)
    blocks = lax.all_to_all(jnp.broadcast_to(block[None], (8, 56, 256)), PIPE, 0, 0, tiled=True)
    shared_grad = jnp.concatenate([blocks[q, :, :SLICE] for q in range(8)], axis=-1).astype(F32)
    shared_gain_grad = summed(blocks[:, :, SLICE], 0)

    lora = terms[:, 512:].astype(BF16)
    lora = lax.all_to_all(jnp.broadcast_to(lora[None], (4, 56, 256)), "z_hi", 0, 0, tiled=True)
    lora = lax.all_to_all(jnp.broadcast_to(lora[:, None], (4, 4, 56, 256)), "y", 1, 1, tiled=True)
    lora = lora.reshape(16, 56, 256)
    lora = jnp.concatenate([lora[..., :128], lora[..., 128:]], axis=1)
    other = swap_cores(lora)
    down_grad = jnp.where(core == 0, lora, other).reshape(WIDTH, RANK)
    up_grad = jnp.where(core == 0, other, lora).reshape(16, 14, 8, 128).swapaxes(1, 2).reshape(RANK, WIDTH)
    return (
        previous.reshape(1, 2, TOK, WIDTH),
        shared_grad,
        shared_gain_grad,
        down_grad[None],
        up_grad[None],
        proj_grad[None],
        mamba_gain[None],
        bias_grad[None],
        decay_grad[None],
    )


def solution(mesh):
    fine = Mesh(mesh.devices.reshape(4, 4, 2, 4, 2), ("z_hi", "y", "core", "x", "z_lo"))
    return jax.shard_map(
        local,
        mesh=fine,
        in_specs=(
            P(PIPE, DP, None, None),
            P(PIPE, DP, None, None),
            P(PIPE, DP, None, None),
            P(DP, None, None),
            P(),
            P(),
            P(PIPE, None, None),
            P(PIPE, None, None),
            P(PIPE, None),
            P(PIPE, None, None),
            P(PIPE, None),
            P(PIPE, None),
        ),
        out_specs=(
            P(PIPE, DP, None, None),
            P(DP, None),
            P(DP),
            P(PIPE, None, None),
            P(PIPE, None, None),
            P(PIPE, DP, None),
            P(PIPE, DP),
            P(PIPE, None),
            P(PIPE, None),
        ),
        check_vma=False,
    )
```

```python
import jax
import jax.numpy as jnp
import numpy as np
from jax import lax
from jax.experimental import pallas as pl
from jax.experimental.pallas import tpu as pltpu
from jax.sharding import Mesh, PartitionSpec as P

EPS = 1e-05
F32 = jnp.float32
BF16 = jnp.bfloat16
HIGHEST = lax.Precision.HIGHEST

WIDTH = 1792
INNER = 3584
RANK = 128
HEADS = 56
TOK = 64
ROWS = 128
CHUNK = 256
CHUNKS = INNER // CHUNK
PART = 448

DP = ("z_hi", "y", "core")
PIPE = ("x", "z_lo")


def nn(a, b):
    return jnp.dot(a, b, preferred_element_type=F32)


def nt(a, b):
    return lax.dot_general(a, b, (((1,), (1,)), ((), ())), preferred_element_type=F32)


def exact(a, b):
    return jnp.dot(a, b, preferred_element_type=F32, precision=HIGHEST)


def two_parts(value):
    high = value.astype(BF16)
    low = (value - high.astype(F32)).astype(BF16)
    return high, low


def lanes_and_rows(shape):
    return lax.broadcasted_iota(jnp.int32, shape, 1), lax.broadcasted_iota(jnp.int32, shape, 0)


def ssd_back(bc, raw, decay_row, expand, gather, head_ref, cot_ref, expanded, stack):
    lane128, _ = lanes_and_rows((TOK, 128))
    low_half = lane128 < TOK
    lane64, row64 = lanes_and_rows((TOK, TOK))
    lower = (row64 >= lane64).astype(F32)
    upper = (row64 <= lane64).astype(F32)
    steps, parts = [], []
    for n in range(2):
        step = jax.nn.softplus(raw[n * TOK : (n + 1) * TOK])
        step = jnp.where(lane128 < HEADS, step, 0.0)
        running = exact(lower, step)
        steps.append(step)
        for value in (running, step):
            first = value.astype(BF16).astype(F32)
            rest = value - first
            second = rest.astype(BF16).astype(F32)
            third = rest - second
            left = jnp.where(low_half, first, pltpu.roll(second, TOK, 1))
            parts.append(jnp.concatenate([left, third], axis=1).astype(BF16))
    expanded[...] = nn(jnp.concatenate(parts, axis=0), expand[...])
    decay_wide = jnp.broadcast_to(decay_row, (8, 128))
    d_first = decay_wide.astype(BF16).astype(F32)
    d_rest = decay_wide - d_first
    d_second = d_rest.astype(BF16).astype(F32)
    lane8, _ = lanes_and_rows((8, 128))
    d_left = jnp.where(lane8 < TOK, d_first, pltpu.roll(d_second, TOK, 1))
    d_parts = jnp.concatenate([d_left, d_rest - d_second], axis=1).astype(BF16)
    decay_lanes = nn(d_parts, expand[...])[0:1]

    lane_c, row_c = lanes_and_rows((TOK, CHUNK))
    token_c = lane_c % TOK
    causal = row_c >= token_c
    diagonal = row_c == token_c
    lane_b, row_b = lanes_and_rows((CHUNK, CHUNK))
    block = (lane_b // TOK) == (row_b // TOK)
    row16 = lax.broadcasted_iota(jnp.int32, (16, CHUNK), 0)
    d_bc = []
    for n in range(2):
        rows = slice(n * TOK, (n + 1) * TOK)
        here = bc[rows]
        rolled = pltpu.roll(here, TOK, 1)
        b_only = jnp.where(low_half, here, 0.0)
        crossing = lax.dot_general(
            rolled,
            jnp.concatenate([b_only] * 4, axis=0),
            (((1,), (1,)), ((), ())),
            preferred_element_type=F32,
            precision=HIGHEST,
        )
        d_cross = jnp.zeros((TOK, CHUNK), F32)
        for g in range(CHUNKS):
            cols = slice(g * CHUNK, (g + 1) * CHUNK)
            heads = jnp.concatenate([head_ref[rows, cols]] * 4, axis=0)
            heads = jnp.where(block, heads, jnp.zeros_like(heads))
            grad = nt(cot_ref[rows, cols], heads)
            run = expanded[n * ROWS : n * ROWS + TOK, cols]
            step = expanded[n * ROWS + TOK : (n + 1) * ROWS, cols]
            run_j = jnp.sum(jnp.where(diagonal, run, 0.0), axis=0, keepdims=True)
            step_j = jnp.sum(jnp.where(diagonal, step, 0.0), axis=0, keepdims=True)
            spread = jnp.where(causal, run - run_j, 0.0)
            kernel = jnp.where(causal, jnp.exp(-decay_lanes[:, cols] * spread), 0.0)
            scored = grad * kernel
            d_cross = d_cross + scored * step_j
            per_step = scored * crossing
            col = jnp.sum(per_step, axis=0, keepdims=True)
            mass = per_step * step_j
            balance = mass - jnp.where(diagonal, col * step_j, 0.0)
            direct = jnp.where(diagonal, col, 0.0)
            spent = jnp.sum(mass * spread, axis=0, keepdims=True)
            base_row = n * 272
            high, low = two_parts(balance)
            stack[base_row : base_row + 64, cols] = high
            stack[base_row + 64 : base_row + 128, cols] = low
            high, low = two_parts(direct)
            stack[base_row + 128 : base_row + 192, cols] = high
            stack[base_row + 192 : base_row + 256, cols] = low
            high = spent.astype(BF16).astype(F32)
            tail = jnp.where(row16 == 0, high, jnp.where(row16 == 1, spent - high, 0.0))
            stack[base_row + 256 : base_row + 272, cols] = tail.astype(BF16)
        d_cross = d_cross[:, :128] + d_cross[:, 128:]
        d_cross = (d_cross + pltpu.roll(d_cross, TOK, 1))[:, :TOK]
        c_low = jnp.where(low_half, rolled, 0.0)
        b_high = jnp.where(low_half, 0.0, rolled)
        d_bc.append(exact(d_cross.T, c_low) + exact(d_cross, b_high))
    gathered = nn(stack[...], gather[...])
    d_raw, decay_cot = [], jnp.zeros((1, 128), F32)
    for n in range(2):
        at = n * 272
        balance = gathered[at : at + 64] + gathered[at + 64 : at + 128]
        direct = gathered[at + 128 : at + 192] + gathered[at + 192 : at + 256]
        spent = jnp.sum(gathered[at + 256 : at + 272], axis=0, keepdims=True)
        d_step = direct + exact(upper, -decay_row * balance)
        d_raw.append(d_step * jax.nn.sigmoid(raw[n * TOK : (n + 1) * TOK]))
        decay_cot = decay_cot - spent
    return jnp.concatenate(d_bc, axis=0), jnp.concatenate(d_raw, axis=0), decay_cot


def front_kernel(
    flags_ref, hidden_any, head_any, cot_any, w_any, down_any, up_any, proj_any, expand_any, gather_any,
    g_ref, mg_ref, bias_ref, decay_ref,
    own_ref, send_ref, normed_t_any, mid_ref, proj_out_any, small_ref,
    normed_t_ref, proj_ref, w_ref, hidden_ref, head_ref, cot_ref, down_ref, up_ref, proj_near, proj_w, expand_ref, gather_ref, expanded, stack, padded, sems,
):
    copies = []
    pairs = (
        (hidden_any, hidden_ref),
        (down_any, down_ref),
        (w_any, w_ref),
        (up_any, up_ref),
        (proj_any, proj_near),
        (expand_any, expand_ref),
        (head_any, head_ref),
        (cot_any, cot_ref),
        (gather_any, gather_ref),
    )
    for k, (source, target) in enumerate(pairs):
        copies.append(pltpu.make_async_copy(source, target, sems.at[k]))
        copies[-1].start()
    padded[...] = jnp.zeros_like(padded)
    padded[0:1, 0:HEADS] = bias_ref[...]
    padded[8:9, 0:HEADS] = decay_ref[...]
    copies[0].wait()
    stream = hidden_ref[...].astype(F32)
    scale0 = lax.rsqrt(jnp.mean(stream * stream, axis=1, keepdims=True) + EPS)
    normed = (stream * scale0 * g_ref[...]).astype(BF16)
    normed_t_ref[...] = normed.T
    copies.append(pltpu.make_async_copy(normed_t_ref, normed_t_any, sems.at[9]))
    copies[9].start()
    copies[1].wait()
    mid = nn(normed, down_ref[...]).astype(BF16)
    mid_ref[...] = mid
    copies[2].wait()
    copies[3].wait()
    act = nn(normed, w_ref[...]) + nn(mid, up_ref[...])
    gate = jax.nn.sigmoid(act)
    slope = gate * (1.0 + act * (1.0 - gate))
    middle = stream + act * gate
    scale1 = lax.rsqrt(jnp.mean(middle * middle, axis=1, keepdims=True) + EPS)
    inner = middle * scale1
    gain = mg_ref[...]
    mamba_in = (inner * gain).astype(BF16)
    for k in range(4, 9):
        copies[k].wait()
    proj_w[...] = jnp.zeros_like(proj_w)
    proj_w[0:184] = proj_near[...]
    bc = nt(mamba_in, proj_w[0:128])
    raw = nt(mamba_in, proj_w[128:256]) + padded[0:1]
    d_bc, d_raw, decay_cot = ssd_back(
        bc, raw, padded[8:9], expand_ref, gather_ref, head_ref, cot_ref, expanded, stack
    )
    d_proj = jnp.concatenate([d_bc.astype(BF16), d_raw.astype(BF16)], axis=1)
    mamba_cot = nn(d_proj, proj_w[...])
    pulled = mamba_cot * inner
    weighted = mamba_cot * gain
    const = scale1 * (weighted - inner * jnp.mean(pulled * gain, axis=1, keepdims=True))
    second = flags_ref[0] == 1
    for k, value in enumerate((const, slope)):
        low, high = value[:TOK].astype(BF16), value[TOK:].astype(BF16)
        own_ref[k] = jnp.where(second, high, low)
        send_ref[k] = jnp.where(second, low, high)
    lane, _ = lanes_and_rows((ROWS, 256))
    ones = jnp.where(lane == 184, 1.0, 0.0).astype(BF16)
    proj_ref[...] = (nn(mamba_in.T, d_proj) + nn(pulled.astype(BF16).T, ones)).astype(BF16)
    _, row8 = lanes_and_rows((8, 128))
    bias_cot = jnp.sum(d_raw, axis=0, keepdims=True)
    small_ref[...] = jnp.where(row8 == 0, bias_cot, jnp.where(row8 == 1, decay_cot, 0.0))
    out = pltpu.make_async_copy(proj_ref, proj_out_any, sems.at[10])
    out.start()
    copies[9].wait()
    out.wait()


def slice_kernel(
    flags_ref, hidden_any, down_any, up_any, hidden_out, down_out, up_out, hidden_near, down_near, up_near, sems
):
    here, core = flags_ref[0], flags_ref[1]
    half = WIDTH // 2
    steps = (
        (hidden_any.at[pl.ds(pl.multiple_of((1 - here) * TOK, TOK), TOK)], hidden_near, hidden_out),
        (down_any.at[pl.ds(pl.multiple_of(core * half, half), half)], down_near, down_out),
        (up_any.at[pl.ds(pl.multiple_of(core * 64, 64), 64)], up_near, up_out),
    )
    first = [pltpu.make_async_copy(source, near, sems.at[k]) for k, (source, near, _) in enumerate(steps)]
    second = [pltpu.make_async_copy(near, target, sems.at[3 + k]) for k, (_, near, target) in enumerate(steps)]
    for copy in first:
        copy.start()
    for one, two in zip(first, second):
        one.wait()
        two.start()
    for copy in second:
        copy.wait()


def base_kernel(flags_ref, hidden_ref, hidden_got_ref, g_ref, base_ref, scale_ref, normed_t_ref):
    here = flags_ref[0]
    later = here == 1
    own = hidden_ref[pl.ds(pl.multiple_of(here * TOK, TOK), TOK), :].astype(F32)
    got = hidden_got_ref[...].astype(F32)
    stream = jnp.concatenate([jnp.where(later, own, got), jnp.where(later, got, own)], axis=0)
    scale0 = lax.rsqrt(jnp.mean(stream * stream, axis=1, keepdims=True) + EPS)
    base = stream * scale0
    base_ref[...] = base
    scale_ref[...] = jnp.broadcast_to(scale0, (ROWS, 128))
    normed_t_ref[...] = (base * g_ref[...]).astype(BF16).T


def wide_kernel(
    flags_ref, w_any, down_ref, up_ref, down_a_ref, down_b_ref, up_a_ref, up_b_ref, wide_ref, w_ref, down_got, up_got, sems
):
    copies = []
    for n in range(WIDTH // 256):
        rows = pl.ds(n * 256, 256)
        copies.append(pltpu.make_async_copy(w_any.at[rows], w_ref.at[rows], sems.at[n]))
        copies[-1].start()
    here, core = flags_ref[0], flags_ref[1]
    half = WIDTH // 2
    down_got[pl.ds(pl.multiple_of(core * half, half), half), :] = down_a_ref[...]
    down_got[pl.ds(pl.multiple_of((1 - core) * half, half), half), :] = down_b_ref[...]
    up_got[pl.ds(pl.multiple_of(core * 64, 64), 64), :] = up_a_ref[...]
    up_got[pl.ds(pl.multiple_of((1 - core) * 64, 64), 64), :] = up_b_ref[...]
    mine, other = 1 - here, here
    own_up, got_up = up_ref[...].T, up_got[...].T
    own_down, got_down = down_ref[...].T, down_got[...].T
    for n in range(WIDTH // 256):
        cols = slice(n * 256, (n + 1) * 256)
        copies[n].wait()
        block = w_ref[cols, :].T.astype(F32)
        wide_ref[mine, :, cols] = (block + nn(own_up, own_down[:, cols])).astype(BF16)
        wide_ref[other, :, cols] = (block + nn(got_up, got_down[:, cols])).astype(BF16)


def section_math(k, arriving, later, own_ref, got_ref, base_ref, scale_ref, wide_ref, g_ref):
    rows = slice(k * TOK, (k + 1) * TOK)
    use_own = later if k == 0 else jnp.logical_not(later)
    const = jnp.where(use_own, own_ref[0], got_ref[0]).astype(F32)
    slope = jnp.where(use_own, own_ref[1], got_ref[1]).astype(F32)
    base = base_ref[rows]
    stream_cot = arriving + const
    act_cot = (stream_cot * slope).astype(BF16)
    normed_cot = nn(act_cot, wide_ref[k])
    pulled = normed_cot * g_ref[...]
    previous = stream_cot + scale_ref[rows, 0:1] * (
        pulled - base * jnp.mean(pulled * base, axis=1, keepdims=True)
    )
    return previous.astype(BF16), act_cot, normed_cot * base


def first_kernel(flags_ref, arriving_ref, *refs):
    previous_ref = refs[-1]
    later = flags_ref[0] == 1
    value = arriving_ref[...]
    for k in range(2):
        value = section_math(k, value.astype(F32), later, *refs[:-1])[0]
    previous_ref[...] = value


def stage_kernel(flags_ref, arriving_ref, total_ref, *refs):
    previous_ref, sum_ref = refs[-2:]
    later = flags_ref[0] == 1
    value = arriving_ref[...]
    sum_ref[...] = (total_ref[...].astype(F32) + value.astype(F32)).astype(BF16)
    for k in range(2):
        value = section_math(k, value.astype(F32), later, *refs[:-2])[0]
    previous_ref[...] = value


def last_kernel(flags_ref, arriving_ref, total_ref, *refs):
    own_prev_ref, back_prev_ref, own_act_ref, back_act_ref, act_ref, shared_gain_ref = refs[-6:]
    later = flags_ref[0] == 1
    value = (arriving_ref[...].astype(F32) + total_ref[...].astype(F32)).astype(BF16)
    previous, acts, gains = [], [], jnp.zeros((1, WIDTH), F32)
    for k in range(2):
        value, act_cot, product = section_math(k, value.astype(F32), later, *refs[:-6])
        previous.append(value)
        acts.append(act_cot)
        gains = gains + jnp.sum(product, axis=0, keepdims=True)
    for pair, own_out, back_out in ((previous, own_prev_ref, back_prev_ref), (acts, own_act_ref, back_act_ref)):
        own_out[...] = jnp.where(later, pair[0], pair[1])
        back_out[...] = jnp.where(later, pair[1], pair[0])
    padded = jnp.concatenate([jnp.concatenate(acts, axis=0), jnp.zeros((ROWS, 128), BF16)], axis=1)
    for q in range(4):
        act_ref[q] = padded[:, q * PART : q * PART + 512]
    shared_gain_ref[...] = gains


def adapter_kernel(flags_ref, own_ref, got_ref, up_ref, normed_t_ref, mid_ref, down_grad_ref, up_grad_ref):
    first = flags_ref[0] == 0
    own, got = own_ref[...], got_ref[...]
    act_cot = jnp.concatenate([jnp.where(first, own, got), jnp.where(first, got, own)], axis=0)
    mid_cot = nt(act_cot, up_ref[...]).astype(BF16)
    down_grad_ref[...] = nn(normed_t_ref[...], mid_cot).astype(BF16)
    up_grad_ref[...] = nn(mid_ref[...].T, act_cot).astype(BF16)


def shared_kernel(flags_ref, all_t_ref, act_own_ref, act_other_ref, out_ref):
    total = jnp.zeros((WIDTH // 2, 512), F32)
    for source in range(4):
        right = jnp.concatenate([act_own_ref[source], act_other_ref[source]], axis=0)
        total = total + nn(all_t_ref[source], right)
    out_ref[...] = total.astype(BF16)


def order_kernel(flags_ref, *refs):
    y, z_hi = flags_ref[3], flags_ref[4]
    out_ref = refs[-1]
    for by, ref in enumerate(refs[:-1]):
        row = jnp.where(y >= by, y - by, y - by + 4)
        for bz in range(4):
            out_ref[jnp.where(z_hi >= bz, z_hi - bz, z_hi - bz + 4) * 4 + row] = ref[bz]


def columns_kernel(flags_ref, *refs):
    x = flags_ref[2]
    shared_ref, gain_ref, blocks = refs[-3:]
    for back, ref in enumerate(refs[:-3]):
        blocks[jnp.where(x >= back, x - back, x - back + 4)] = ref[...].astype(F32)
    parts, gain = [], jnp.zeros((56, 1), F32)
    for q in range(4):
        block = blocks[q]
        parts.append(block[:, :PART])
        gain = gain + block[:, PART : PART + 1]
    shared_ref[...] = jnp.concatenate(parts, axis=1)
    gain_ref[...] = jnp.broadcast_to(gain, (56, 128))


def shape(dims, dtype):
    return jax.ShapeDtypeStruct(dims, dtype)


def call(kernel, outs, megabytes, args, scratch=(), copied=(), out_copied=()):
    place = lambda k, chosen: pl.BlockSpec(memory_space=pltpu.HBM) if k in chosen else pl.BlockSpec()
    return pl.pallas_call(
        kernel,
        out_shape=tuple(outs),
        in_specs=[pl.BlockSpec(memory_space=pltpu.SMEM)] + [place(k, copied) for k in range(1, len(args))],
        out_specs=tuple(place(k, out_copied) for k in range(len(outs))),
        scratch_shapes=list(scratch),
        compiler_params=pltpu.CompilerParams(vmem_limit_bytes=megabytes * 1024 * 1024),
        cost_estimate=pl.CostEstimate(flops=1_000, bytes_accessed=1_000, transcendentals=0),
    )(*args)


def one_hots():
    rows = np.arange(256)[:, None]
    lanes = np.arange(INNER)[None, :]
    expand = ((rows < 192) & (rows % TOK == lanes // TOK)).astype(np.float32)
    gather = (np.arange(INNER)[:, None] // TOK == np.arange(128)[None, :]).astype(np.float32)
    return jnp.asarray(expand, BF16), jnp.asarray(gather, BF16)


def swap(value, axis):
    return lax.ppermute(value, axis, [(0, 1), (1, 0)])


def pick(value, index, axis=0):
    return lax.dynamic_index_in_dim(value, index, axis, keepdims=False, allow_negative_indices=False)


def shifted(value, axis, by):
    return lax.ppermute(value, axis, [(i, (i + by) % 4) for i in range(4)])


def scattered_sum(value, axis, places):
    total = pick(value, places[0]).astype(F32)
    for by in range(1, 4):
        total = total + shifted(pick(value, places[by]), axis, by).astype(F32)
    return total


def summed(value, axis):
    return jnp.sum(value.astype(F32), axis=axis)


def after(value, *others):
    return lax.optimization_barrier((value, *others))[0]


def local(hidden, heads, cots, final, w, g, down, up, mg, proj_w, bias, decay):
    core, x, z_lo = lax.axis_index("core"), lax.axis_index("x"), lax.axis_index("z_lo")
    y, z_hi = lax.axis_index("y"), lax.axis_index("z_hi")
    flags = jnp.stack([z_lo, core, x, y, z_hi]).astype(jnp.int32)
    y_places = [y] + [jnp.where(y + by < 4, y + by, y + by - 4) for by in range(1, 4)]
    z_places = [z_hi] + [jnp.where(z_hi + by < 4, z_hi + by, z_hi + by - 4) for by in range(1, 4)]
    first_core, first_z, last_x = core == 0, z_lo == 0, x == 3
    down, up = down[0], up[0]
    hidden, heads, cots = (a[0].reshape(ROWS, a.shape[-1]) for a in (hidden, heads, cots))
    flags, y_places, z_places, core, other_core, z_lo, first_core, first_z, last_x, hidden = lax.optimization_barrier(
        (flags, y_places, z_places, core, 1 - core, z_lo, first_core, first_z, last_x, hidden)
    )
    g_row = g[None]
    row = shape((TOK, WIDTH), BF16)
    dma = pltpu.SemaphoreType.DMA

    hidden_send, down_send, up_send = call(
        slice_kernel,
        (row, shape((WIDTH // 2, RANK), BF16), shape((64, WIDTH), BF16)),
        60,
        (flags, hidden, down, up),
        [
            pltpu.VMEM((TOK, WIDTH), BF16),
            pltpu.VMEM((WIDTH // 2, RANK), BF16),
            pltpu.VMEM((64, WIDTH), BF16),
            dma((6,)),
        ],
        (1, 2, 3),
        (0, 1, 2),
    )
    hidden_got = swap(hidden_send, "z_lo")
    down_a, up_a = swap(down_send, "z_lo"), swap(up_send, "z_lo")
    down_b, up_b = swap(down_a, "core"), swap(up_a, "core")

    expand, gather = one_hots()
    scratch = [
        pltpu.VMEM((WIDTH, ROWS), BF16),
        pltpu.VMEM((WIDTH, 256), BF16),
        pltpu.VMEM((WIDTH, WIDTH), BF16),
        pltpu.VMEM((ROWS, WIDTH), BF16),
        pltpu.VMEM((ROWS, INNER), BF16),
        pltpu.VMEM((ROWS, INNER), BF16),
        pltpu.VMEM((WIDTH, RANK), BF16),
        pltpu.VMEM((RANK, WIDTH), BF16),
        pltpu.VMEM((184, WIDTH), BF16),
        pltpu.VMEM((256, WIDTH), BF16),
        pltpu.VMEM((256, INNER), BF16),
        pltpu.VMEM((INNER, 128), BF16),
        pltpu.VMEM((256, INNER), F32),
        pltpu.VMEM((544, INNER), BF16),
        pltpu.VMEM((16, 128), F32),
        dma((11,)),
    ]
    own, send, normed_t, mid, proj_part, small = call(
        front_kernel,
        (
            shape((2, TOK, WIDTH), BF16),
            shape((2, TOK, WIDTH), BF16),
            shape((WIDTH, ROWS), BF16),
            shape((ROWS, RANK), BF16),
            shape((WIDTH, 256), BF16),
            shape((8, 128), F32),
        ),
        60,
        (flags, hidden, heads, cots, w, down, up, proj_w[0].T, expand, gather, g_row, mg, bias, decay),
        scratch,
        range(1, 10),
        (2, 4),
    )
    got = swap(send, "z_lo")

    base, scale, pair_t = call(
        base_kernel,
        (shape((ROWS, WIDTH), F32), shape((ROWS, 128), F32), shape((WIDTH, ROWS), BF16)),
        8,
        (flags, after(hidden, small, down_a, up_a), hidden_got, g_row),
    )
    pair_t = pair_t.reshape(16, 2, 56, ROWS)
    pair_t = jnp.concatenate([pick(pair_t, core, 1), swap(pick(pair_t, other_core, 1), "core")], -1).reshape(896, 256)
    all_t = lax.all_gather(pair_t, "x", axis=0, tiled=False)

    lane = lax.broadcasted_iota(jnp.int32, (32, 56, 256), 2)
    heads_col = lambda v: v[:HEADS].astype(BF16)[None, :, None]
    proj_part, small, _ = lax.optimization_barrier((proj_part, small, pair_t))
    proj_part = proj_part.reshape(32, 56, 256)
    proj_part = jnp.where(lane == 186, heads_col(small[0]), proj_part)
    proj_part = jnp.where(lane == 187, heads_col(small[1]), proj_part)
    proj_part = proj_part.reshape(16, 2, 56, 256)
    proj_part = pick(proj_part, core, 1).astype(F32) + swap(pick(proj_part, other_core, 1), "core").astype(F32)
    proj_part = proj_part.astype(BF16).reshape(4, 4, 56, 256).swapaxes(0, 1)

    (w_both,) = call(
        wide_kernel,
        (shape((2, WIDTH, WIDTH), BF16),),
        24,
        (flags, after(w, pair_t, proj_part), down, up, down_a, down_b, up_a, up_b),
        [
            pltpu.VMEM((WIDTH, WIDTH), BF16),
            pltpu.VMEM((WIDTH, RANK), BF16),
            pltpu.VMEM((RANK, WIDTH), BF16),
            dma((7,)),
        ],
        (1,),
    )

    arriving = jnp.where(last_x, pick(final, z_lo), jnp.zeros((TOK, WIDTH), BF16))
    rest = (own, got, base, scale, w_both, g_row)
    total = arriving
    for tick in range(3):
        if tick == 0:
            (previous,) = call(first_kernel, (row,), 8, (flags, arriving, *rest))
        else:
            previous, total = call(stage_kernel, (row, row), 8, (flags, arriving, total, *rest))
        arriving = lax.ppermute(previous, "x", [(3 - tick, 2 - tick)])
    own_prev, back_prev, own_act, back_act, act, shared_gain = call(
        last_kernel,
        (row, row, row, row, shape((4, ROWS, 512), BF16), shape((1, WIDTH), F32)),
        14,
        (flags, arriving, total, *rest),
    )
    got_act = swap(back_act, "z_lo")
    got_prev = swap(back_prev, "z_lo")

    proj_sum = scattered_sum(after(proj_part, own_act), "y", y_places).astype(BF16)
    proj_sum = jnp.concatenate([proj_sum[..., :128], proj_sum[..., 128:]], axis=1)

    act_own = lax.all_to_all(act, "x", 0, 0, tiled=True)
    act_other = swap(act_own, "core")
    lora_down, lora_up = call(
        adapter_kernel,
        (shape((WIDTH, RANK), BF16), shape((RANK, WIDTH), BF16)),
        10,
        (flags, own_act, got_act, up, normed_t, mid),
    )
    down_tiles = lora_down.reshape(16, 112, 128)
    up_tiles = lora_up.reshape(16, 8, 14, 128).swapaxes(1, 2).reshape(16, 112, 128)
    own_l = jnp.where(first_core, down_tiles, up_tiles)
    other_l = jnp.where(first_core, up_tiles, down_tiles)
    lora = own_l.astype(F32) + swap(other_l, "core").astype(F32)
    gain_col = shared_gain.reshape(16, 2, 56)
    gain_col = pick(gain_col, core, 1) + swap(pick(gain_col, other_core, 1), "core")
    (shared,) = call(shared_kernel, (shape((896, 512), BF16),), 12, (flags, after(all_t, proj_sum), act_own, act_other))
    lane = lax.broadcasted_iota(jnp.int32, (16, 56, 512), 2)
    shared = jnp.where(lane == PART, gain_col.astype(BF16)[..., None], shared.reshape(16, 56, 512))
    shared = jnp.concatenate([shared[..., :256], shared[..., 256:]], axis=1)
    terms = jnp.concatenate([shared, lora.astype(BF16)], axis=-1).reshape(4, 4, 112, 384)
    terms = summed(lax.all_to_all(terms, "y", 1, 1, tiled=True), 1).astype(BF16)
    terms = scattered_sum(jnp.concatenate([terms, proj_sum], axis=-1), "z_hi", z_places)
    proj_sum = jnp.concatenate([terms[:56, 384:], terms[56:, 384:]], axis=1)
    terms = terms.astype(BF16)

    lora = terms[:, 256:384]
    lora = jnp.stack([lora] + [shifted(lora, "z_hi", by) for by in range(1, 4)])
    block = jnp.concatenate([terms[:56, :256], terms[56:, :256]], axis=1)
    block = (block.astype(F32) + swap(block, "z_lo").astype(F32)).astype(BF16)
    lora, block = lax.optimization_barrier((lora, block))
    lora = [lora] + [shifted(lora, "y", by) for by in range(1, 4)]
    block = [block] + [shifted(block, "x", by) for by in range(1, 4)]
    lora[0] = after(lora[0], *block)
    shared_grad, shared_gain_grad = call(
        columns_kernel,
        (shape((56, WIDTH), F32), shape((56, 128), F32)),
        8,
        (flags, *block),
        [pltpu.VMEM((4, 56, 512), F32)],
    )
    (lora,) = call(order_kernel, (shape((16, 112, 128), BF16),), 8, (flags, *lora))
    other = swap(lora, "core")
    down_grad = jnp.where(first_core, lora, other).reshape(WIDTH, RANK)
    up_grad = jnp.where(first_core, other, lora).reshape(16, 14, 8, 128).swapaxes(1, 2).reshape(RANK, WIDTH)
    section_grad = jnp.where(first_z, jnp.stack([own_prev, got_prev]), jnp.stack([got_prev, own_prev]))
    return (
        section_grad[None],
        shared_grad,
        shared_gain_grad[:, 0],
        down_grad[None],
        up_grad[None],
        proj_sum[None, :, :184],
        proj_sum[None, :, 184],
        proj_sum[None, :, 186],
        proj_sum[None, :, 187],
    )


def solution(mesh):
    fine = Mesh(mesh.devices.reshape(4, 4, 2, 4, 2), ("z_hi", "y", "core", "x", "z_lo"))
    return jax.shard_map(
        local,
        mesh=fine,
        in_specs=(
            P(PIPE, DP, None, None),
            P(PIPE, DP, None, None),
            P(PIPE, DP, None, None),
            P(DP, None, None),
            P(),
            P(),
            P(PIPE, None, None),
            P(PIPE, None, None),
            P(PIPE, None),
            P(PIPE, None, None),
            P(PIPE, None),
            P(PIPE, None),
        ),
        out_specs=(
            P(PIPE, DP, None, None),
            P(DP, None),
            P(DP),
            P(PIPE, None, None),
            P(PIPE, None, None),
            P(PIPE, DP, None),
            P(PIPE, DP),
            P(PIPE, None),
            P(PIPE, None),
        ),
        check_vma=False,
    )
```

```python
import jax
import jax.numpy as jnp
import numpy as np
from jax import lax
from jax.experimental import pallas as pl
from jax.experimental.pallas import tpu as pltpu
from jax.sharding import Mesh, PartitionSpec as P

EPS = 1e-05
F32 = jnp.float32
BF16 = jnp.bfloat16
HIGHEST = lax.Precision.HIGHEST

WIDTH = 1792
INNER = 3584
RANK = 128
HEADS = 56
TOK = 64
ROWS = 128
CHUNK = 256
CHUNKS = INNER // CHUNK
PART = 448

DP = ("z_hi", "y", "core")
PIPE = ("x", "z_lo")


def nn(a, b):
    return jnp.dot(a, b, preferred_element_type=F32)


def nt(a, b):
    return lax.dot_general(a, b, (((1,), (1,)), ((), ())), preferred_element_type=F32)


def exact(a, b):
    return jnp.dot(a, b, preferred_element_type=F32, precision=HIGHEST)


def two_parts(value):
    high = value.astype(BF16)
    low = (value - high.astype(F32)).astype(BF16)
    return high, low


def lanes_and_rows(shape):
    return lax.broadcasted_iota(jnp.int32, shape, 1), lax.broadcasted_iota(jnp.int32, shape, 0)


def ssd_back(bc, raw, decay_row, expand, gather, head_ref, cot_ref, expanded, stack):
    lane128, _ = lanes_and_rows((TOK, 128))
    low_half = lane128 < TOK
    lane64, row64 = lanes_and_rows((TOK, TOK))
    lower = (row64 >= lane64).astype(F32)
    upper = (row64 <= lane64).astype(F32)
    steps, parts = [], []
    for n in range(2):
        step = jax.nn.softplus(raw[n * TOK : (n + 1) * TOK])
        step = jnp.where(lane128 < HEADS, step, 0.0)
        running = exact(lower, step)
        steps.append(step)
        for value in (running, step):
            first = value.astype(BF16).astype(F32)
            rest = value - first
            second = rest.astype(BF16).astype(F32)
            third = rest - second
            left = jnp.where(low_half, first, pltpu.roll(second, TOK, 1))
            parts.append(jnp.concatenate([left, third], axis=1).astype(BF16))
    expanded[...] = nn(jnp.concatenate(parts, axis=0), expand[...])
    decay_wide = jnp.broadcast_to(decay_row, (8, 128))
    d_first = decay_wide.astype(BF16).astype(F32)
    d_rest = decay_wide - d_first
    d_second = d_rest.astype(BF16).astype(F32)
    lane8, _ = lanes_and_rows((8, 128))
    d_left = jnp.where(lane8 < TOK, d_first, pltpu.roll(d_second, TOK, 1))
    d_parts = jnp.concatenate([d_left, d_rest - d_second], axis=1).astype(BF16)
    decay_lanes = nn(d_parts, expand[...])[0:1]

    lane_c, row_c = lanes_and_rows((TOK, CHUNK))
    token_c = lane_c % TOK
    causal = row_c >= token_c
    diagonal = row_c == token_c
    lane_b, row_b = lanes_and_rows((CHUNK, CHUNK))
    block = (lane_b // TOK) == (row_b // TOK)
    row16 = lax.broadcasted_iota(jnp.int32, (16, CHUNK), 0)
    d_bc = []
    for n in range(2):
        rows = slice(n * TOK, (n + 1) * TOK)
        here = bc[rows]
        rolled = pltpu.roll(here, TOK, 1)
        b_only = jnp.where(low_half, here, 0.0)
        crossing = lax.dot_general(
            rolled,
            jnp.concatenate([b_only] * 4, axis=0),
            (((1,), (1,)), ((), ())),
            preferred_element_type=F32,
            precision=HIGHEST,
        )
        d_cross = jnp.zeros((TOK, CHUNK), F32)
        for g in range(CHUNKS):
            cols = slice(g * CHUNK, (g + 1) * CHUNK)
            heads = jnp.concatenate([head_ref[rows, cols]] * 4, axis=0)
            heads = jnp.where(block, heads, jnp.zeros_like(heads))
            grad = nt(cot_ref[rows, cols], heads)
            run = expanded[n * ROWS : n * ROWS + TOK, cols]
            step = expanded[n * ROWS + TOK : (n + 1) * ROWS, cols]
            run_j = jnp.sum(jnp.where(diagonal, run, 0.0), axis=0, keepdims=True)
            step_j = jnp.sum(jnp.where(diagonal, step, 0.0), axis=0, keepdims=True)
            spread = jnp.where(causal, run - run_j, 0.0)
            kernel = jnp.where(causal, jnp.exp(-decay_lanes[:, cols] * spread), 0.0)
            scored = grad * kernel
            d_cross = d_cross + scored * step_j
            per_step = scored * crossing
            col = jnp.sum(per_step, axis=0, keepdims=True)
            mass = per_step * step_j
            balance = mass - jnp.where(diagonal, col * step_j, 0.0)
            direct = jnp.where(diagonal, col, 0.0)
            spent = jnp.sum(mass * spread, axis=0, keepdims=True)
            base_row = n * 272
            high, low = two_parts(balance)
            stack[base_row : base_row + 64, cols] = high
            stack[base_row + 64 : base_row + 128, cols] = low
            high, low = two_parts(direct)
            stack[base_row + 128 : base_row + 192, cols] = high
            stack[base_row + 192 : base_row + 256, cols] = low
            high = spent.astype(BF16).astype(F32)
            tail = jnp.where(row16 == 0, high, jnp.where(row16 == 1, spent - high, 0.0))
            stack[base_row + 256 : base_row + 272, cols] = tail.astype(BF16)
        d_cross = d_cross[:, :128] + d_cross[:, 128:]
        d_cross = (d_cross + pltpu.roll(d_cross, TOK, 1))[:, :TOK]
        c_low = jnp.where(low_half, rolled, 0.0)
        b_high = jnp.where(low_half, 0.0, rolled)
        d_bc.append(exact(d_cross.T, c_low) + exact(d_cross, b_high))
    gathered = nn(stack[...], gather[...])
    d_raw, decay_cot = [], jnp.zeros((1, 128), F32)
    for n in range(2):
        at = n * 272
        balance = gathered[at : at + 64] + gathered[at + 64 : at + 128]
        direct = gathered[at + 128 : at + 192] + gathered[at + 192 : at + 256]
        spent = jnp.sum(gathered[at + 256 : at + 272], axis=0, keepdims=True)
        d_step = direct + exact(upper, -decay_row * balance)
        d_raw.append(d_step * jax.nn.sigmoid(raw[n * TOK : (n + 1) * TOK]))
        decay_cot = decay_cot - spent
    return jnp.concatenate(d_bc, axis=0), jnp.concatenate(d_raw, axis=0), decay_cot


def front_kernel(
    flags_ref, hidden_any, head_any, cot_any, w_any, down_any, up_any, proj_any, expand_any, gather_any, repeat_any,
    g_ref, mg_ref, bias_ref, decay_ref,
    own_ref, send_ref, normed_t_any, mid_ref, proj_out_any,
    normed_t_ref, proj_ref, w_ref, hidden_ref, head_ref, cot_ref, down_ref, up_ref, proj_near, proj_w, expand_ref, gather_ref, repeat_ref, expanded, stack, padded, sems,
):
    copies = []
    pairs = (
        (hidden_any, hidden_ref),
        (down_any, down_ref),
        (w_any, w_ref),
        (up_any, up_ref),
        (proj_any, proj_near),
        (expand_any, expand_ref),
        (head_any, head_ref),
        (cot_any, cot_ref),
        (gather_any, gather_ref),
        (repeat_any, repeat_ref),
    )
    for k, (source, target) in enumerate(pairs):
        copies.append(pltpu.make_async_copy(source, target, sems.at[k]))
        copies[-1].start()
    padded[...] = jnp.zeros_like(padded)
    padded[0:1, 0:HEADS] = bias_ref[...]
    padded[8:9, 0:HEADS] = decay_ref[...]
    copies[0].wait()
    stream = hidden_ref[...].astype(F32)
    scale0 = lax.rsqrt(jnp.mean(stream * stream, axis=1, keepdims=True) + EPS)
    normed = (stream * scale0 * g_ref[...]).astype(BF16)
    normed_t_ref[...] = normed.T
    copies.append(pltpu.make_async_copy(normed_t_ref, normed_t_any, sems.at[10]))
    copies[10].start()
    copies[1].wait()
    mid = nn(normed, down_ref[...]).astype(BF16)
    mid_ref[...] = mid
    copies[2].wait()
    copies[3].wait()
    act = nn(normed, w_ref[...]) + nn(mid, up_ref[...])
    gate = jax.nn.sigmoid(act)
    slope = gate * (1.0 + act * (1.0 - gate))
    middle = stream + act * gate
    scale1 = lax.rsqrt(jnp.mean(middle * middle, axis=1, keepdims=True) + EPS)
    inner = middle * scale1
    gain = mg_ref[...]
    mamba_in = (inner * gain).astype(BF16)
    for k in range(4, 10):
        copies[k].wait()
    proj_w[...] = jnp.zeros_like(proj_w)
    proj_w[0:184] = proj_near[...]
    bc = nt(mamba_in, proj_w[0:128])
    raw = nt(mamba_in, proj_w[128:256]) + padded[0:1]
    d_bc, d_raw, decay_cot = ssd_back(
        bc, raw, padded[8:9], expand_ref, gather_ref, head_ref, cot_ref, expanded, stack
    )
    d_proj = jnp.concatenate([d_bc.astype(BF16), d_raw.astype(BF16)], axis=1)
    mamba_cot = nn(d_proj, proj_w[...])
    pulled = mamba_cot * inner
    weighted = mamba_cot * gain
    const = scale1 * (weighted - inner * jnp.mean(pulled * gain, axis=1, keepdims=True))
    second = flags_ref[0] == 1
    for k, value in enumerate((const, slope)):
        low, high = value[:TOK].astype(BF16), value[TOK:].astype(BF16)
        own_ref[k] = jnp.where(second, high, low)
        send_ref[k] = jnp.where(second, low, high)
    lane, row = lanes_and_rows((ROWS, 256))
    ones = jnp.where(lane == 184, 1.0, 0.0).astype(BF16)
    small = jnp.concatenate(
        [jnp.sum(d_raw, axis=0, keepdims=True), decay_cot, jnp.zeros((6, 128), F32)], axis=0
    ).T
    small = jnp.where(lane == 186, small[:, 0:1], jnp.where(lane == 187, small[:, 1:2], 0.0)).astype(BF16)
    proj_ref[...] = (
        nn(mamba_in.T, d_proj) + nn(pulled.astype(BF16).T, ones) + nn(repeat_ref[...], small)
    ).astype(BF16)
    out = pltpu.make_async_copy(proj_ref, proj_out_any, sems.at[11])
    out.start()
    copies[10].wait()
    out.wait()


def slice_kernel(
    flags_ref, hidden_any, down_any, up_any, hidden_out, down_out, up_out, hidden_near, down_near, up_near, sems
):
    here, core = flags_ref[0], flags_ref[1]
    half = WIDTH // 2
    steps = (
        (hidden_any.at[pl.ds(pl.multiple_of((1 - here) * TOK, TOK), TOK)], hidden_near, hidden_out),
        (down_any.at[pl.ds(pl.multiple_of(core * half, half), half)], down_near, down_out),
        (up_any.at[pl.ds(pl.multiple_of(core * 64, 64), 64)], up_near, up_out),
    )
    first = [pltpu.make_async_copy(source, near, sems.at[k]) for k, (source, near, _) in enumerate(steps)]
    second = [pltpu.make_async_copy(near, target, sems.at[3 + k]) for k, (_, near, target) in enumerate(steps)]
    for copy in first:
        copy.start()
    for one, two in zip(first, second):
        one.wait()
        two.start()
    for copy in second:
        copy.wait()


def base_kernel(flags_ref, hidden_ref, hidden_got_ref, g_ref, base_ref, scale_ref, normed_t_ref):
    here = flags_ref[0]
    later = here == 1
    own = hidden_ref[pl.ds(pl.multiple_of(here * TOK, TOK), TOK), :].astype(F32)
    got = hidden_got_ref[...].astype(F32)
    stream = jnp.concatenate([jnp.where(later, own, got), jnp.where(later, got, own)], axis=0)
    scale0 = lax.rsqrt(jnp.mean(stream * stream, axis=1, keepdims=True) + EPS)
    base = stream * scale0
    base_ref[...] = base
    scale_ref[...] = jnp.broadcast_to(scale0, (ROWS, 128))
    normed_t_ref[...] = (base * g_ref[...]).astype(BF16).T


def wide_kernel(
    flags_ref, w_any, down_ref, up_ref, down_a_ref, down_b_ref, up_a_ref, up_b_ref, wide_ref, w_ref, down_got, up_got, sems
):
    copies = []
    for n in range(WIDTH // 256):
        rows = pl.ds(n * 256, 256)
        copies.append(pltpu.make_async_copy(w_any.at[rows], w_ref.at[rows], sems.at[n]))
        copies[-1].start()
    here, core = flags_ref[0], flags_ref[1]
    half = WIDTH // 2
    down_got[pl.ds(pl.multiple_of(core * half, half), half), :] = down_a_ref[...]
    down_got[pl.ds(pl.multiple_of((1 - core) * half, half), half), :] = down_b_ref[...]
    up_got[pl.ds(pl.multiple_of(core * 64, 64), 64), :] = up_a_ref[...]
    up_got[pl.ds(pl.multiple_of((1 - core) * 64, 64), 64), :] = up_b_ref[...]
    mine, other = 1 - here, here
    own_up, got_up = up_ref[...].T, up_got[...].T
    own_down, got_down = down_ref[...].T, down_got[...].T
    for n in range(WIDTH // 256):
        cols = slice(n * 256, (n + 1) * 256)
        copies[n].wait()
        block = w_ref[cols, :].T.astype(F32)
        wide_ref[mine, :, cols] = (block + nn(own_up, own_down[:, cols])).astype(BF16)
        wide_ref[other, :, cols] = (block + nn(got_up, got_down[:, cols])).astype(BF16)


def section_math(k, arriving, later, own_ref, got_ref, base_ref, scale_ref, wide_ref, g_ref):
    rows = slice(k * TOK, (k + 1) * TOK)
    use_own = later if k == 0 else jnp.logical_not(later)
    const = jnp.where(use_own, own_ref[0], got_ref[0]).astype(F32)
    slope = jnp.where(use_own, own_ref[1], got_ref[1]).astype(F32)
    base = base_ref[rows]
    stream_cot = arriving + const
    act_cot = (stream_cot * slope).astype(BF16)
    normed_cot = nn(act_cot, wide_ref[k])
    pulled = normed_cot * g_ref[...]
    previous = stream_cot + scale_ref[rows, 0:1] * (
        pulled - base * jnp.mean(pulled * base, axis=1, keepdims=True)
    )
    return previous.astype(BF16), act_cot, normed_cot * base


def first_kernel(flags_ref, arriving_ref, *refs):
    previous_ref = refs[-1]
    later = flags_ref[0] == 1
    value = arriving_ref[...]
    for k in range(2):
        value = section_math(k, value.astype(F32), later, *refs[:-1])[0]
    previous_ref[...] = value


def stage_kernel(flags_ref, arriving_ref, total_ref, *refs):
    previous_ref, sum_ref = refs[-2:]
    later = flags_ref[0] == 1
    value = arriving_ref[...]
    sum_ref[...] = (total_ref[...].astype(F32) + value.astype(F32)).astype(BF16)
    for k in range(2):
        value = section_math(k, value.astype(F32), later, *refs[:-2])[0]
    previous_ref[...] = value


def last_kernel(flags_ref, arriving_ref, total_ref, *refs):
    own_prev_ref, back_prev_ref, own_act_ref, back_act_ref, act_ref, shared_gain_ref = refs[-6:]
    later = flags_ref[0] == 1
    value = (arriving_ref[...].astype(F32) + total_ref[...].astype(F32)).astype(BF16)
    previous, acts, gains = [], [], jnp.zeros((1, WIDTH), F32)
    for k in range(2):
        value, act_cot, product = section_math(k, value.astype(F32), later, *refs[:-6])
        previous.append(value)
        acts.append(act_cot)
        gains = gains + jnp.sum(product, axis=0, keepdims=True)
    for pair, own_out, back_out in ((previous, own_prev_ref, back_prev_ref), (acts, own_act_ref, back_act_ref)):
        own_out[...] = jnp.where(later, pair[0], pair[1])
        back_out[...] = jnp.where(later, pair[1], pair[0])
    padded = jnp.concatenate([jnp.concatenate(acts, axis=0), jnp.zeros((ROWS, 128), BF16)], axis=1)
    for q in range(4):
        act_ref[q] = padded[:, q * PART : q * PART + 512]
    shared_gain_ref[...] = gains


def adapter_kernel(flags_ref, own_ref, got_ref, up_ref, normed_t_ref, mid_ref, down_grad_ref, up_grad_ref):
    first = flags_ref[0] == 0
    own, got = own_ref[...], got_ref[...]
    act_cot = jnp.concatenate([jnp.where(first, own, got), jnp.where(first, got, own)], axis=0)
    mid_cot = nt(act_cot, up_ref[...]).astype(BF16)
    down_grad_ref[...] = nn(normed_t_ref[...], mid_cot).astype(BF16)
    up_grad_ref[...] = nn(mid_ref[...].T, act_cot).astype(BF16)


def shared_kernel(flags_ref, t0_ref, t1_ref, t2_ref, t3_ref, act_own_ref, act_other_ref, out_ref):
    x = flags_ref[2]
    total = jnp.zeros((WIDTH // 2, 512), F32)
    for back, ref in enumerate((t0_ref, t1_ref, t2_ref, t3_ref)):
        source = jnp.where(x >= back, x - back, x - back + 4)
        right = jnp.concatenate([act_own_ref[source], act_other_ref[source]], axis=0)
        total = total + nn(ref[...], right)
    out_ref[...] = total.astype(BF16)


def order_kernel(flags_ref, *refs):
    y, z_hi = flags_ref[3], flags_ref[4]
    out_ref = refs[-1]
    for by, ref in enumerate(refs[:-1]):
        row = jnp.where(y >= by, y - by, y - by + 4)
        for bz in range(4):
            out_ref[jnp.where(z_hi >= bz, z_hi - bz, z_hi - bz + 4) * 4 + row] = ref[bz]


def columns_kernel(flags_ref, *refs):
    x = flags_ref[2]
    shared_ref, gain_ref, blocks = refs[-3:]
    for back, ref in enumerate(refs[:-3]):
        blocks[jnp.where(x >= back, x - back, x - back + 4)] = ref[...].astype(F32)
    parts, gain = [], jnp.zeros((56, 1), F32)
    for q in range(4):
        block = blocks[q]
        parts.append(block[:, :PART])
        gain = gain + block[:, PART : PART + 1]
    shared_ref[...] = jnp.concatenate(parts, axis=1)
    gain_ref[...] = jnp.broadcast_to(gain, (56, 128))


def shape(dims, dtype):
    return jax.ShapeDtypeStruct(dims, dtype)


def call(kernel, outs, megabytes, args, scratch=(), copied=(), out_copied=()):
    place = lambda k, chosen: pl.BlockSpec(memory_space=pltpu.HBM) if k in chosen else pl.BlockSpec()
    return pl.pallas_call(
        kernel,
        out_shape=tuple(outs),
        in_specs=[pl.BlockSpec(memory_space=pltpu.SMEM)] + [place(k, copied) for k in range(1, len(args))],
        out_specs=tuple(place(k, out_copied) for k in range(len(outs))),
        scratch_shapes=list(scratch),
        compiler_params=pltpu.CompilerParams(vmem_limit_bytes=megabytes * 1024 * 1024),
        cost_estimate=pl.CostEstimate(flops=1_000, bytes_accessed=1_000, transcendentals=0),
    )(*args)


def one_hots():
    rows = np.arange(256)[:, None]
    lanes = np.arange(INNER)[None, :]
    expand = ((rows < 192) & (rows % TOK == lanes // TOK)).astype(np.float32)
    gather = (np.arange(INNER)[:, None] // TOK == np.arange(128)[None, :]).astype(np.float32)
    repeat = (np.arange(WIDTH)[:, None] % HEADS == np.arange(128)[None, :]).astype(np.float32)
    return jnp.asarray(expand, BF16), jnp.asarray(gather, BF16), jnp.asarray(repeat, BF16)


def swap(value, axis):
    return lax.ppermute(value, axis, [(0, 1), (1, 0)])


def pick(value, index, axis=0):
    return lax.dynamic_index_in_dim(value, index, axis, keepdims=False, allow_negative_indices=False)


def shifted(value, axis, by):
    return lax.ppermute(value, axis, [(i, (i + by) % 4) for i in range(4)])


def scattered_sum(value, axis, places):
    total = pick(value, places[0]).astype(F32)
    for by in range(1, 4):
        total = total + shifted(pick(value, places[by]), axis, by).astype(F32)
    return total


def summed(value, axis):
    return jnp.sum(value.astype(F32), axis=axis)


def hold(*values):
    return lax.optimization_barrier(values)


def local(hidden, heads, cots, final, w, g, down, up, mg, proj_w, bias, decay):
    core, x, z_lo = lax.axis_index("core"), lax.axis_index("x"), lax.axis_index("z_lo")
    y, z_hi = lax.axis_index("y"), lax.axis_index("z_hi")
    flags = jnp.stack([z_lo, core, x, y, z_hi]).astype(jnp.int32)
    y_places = [y] + [jnp.where(y + by < 4, y + by, y + by - 4) for by in range(1, 4)]
    z_places = [z_hi] + [jnp.where(z_hi + by < 4, z_hi + by, z_hi + by - 4) for by in range(1, 4)]
    first_core, first_z, last_x = core == 0, z_lo == 0, x == 3
    down, up = down[0], up[0]
    hidden, heads, cots = (a[0].reshape(ROWS, a.shape[-1]) for a in (hidden, heads, cots))
    flags, y_places, z_places, core, other_core, z_lo, first_core, first_z, last_x, hidden = lax.optimization_barrier(
        (flags, y_places, z_places, core, 1 - core, z_lo, first_core, first_z, last_x, hidden)
    )
    g_row = g[None]
    row = shape((TOK, WIDTH), BF16)
    dma = pltpu.SemaphoreType.DMA

    hidden_send, down_send, up_send = call(
        slice_kernel,
        (row, shape((WIDTH // 2, RANK), BF16), shape((64, WIDTH), BF16)),
        60,
        (flags, hidden, down, up),
        [
            pltpu.VMEM((TOK, WIDTH), BF16),
            pltpu.VMEM((WIDTH // 2, RANK), BF16),
            pltpu.VMEM((64, WIDTH), BF16),
            dma((6,)),
        ],
        (1, 2, 3),
        (0, 1, 2),
    )
    hidden_got = swap(hidden_send, "z_lo")
    down_a, up_a = swap(down_send, "z_lo"), swap(up_send, "z_lo")

    expand, gather, repeat = one_hots()
    scratch = [
        pltpu.VMEM((WIDTH, ROWS), BF16),
        pltpu.VMEM((WIDTH, 256), BF16),
        pltpu.VMEM((WIDTH, WIDTH), BF16),
        pltpu.VMEM((ROWS, WIDTH), BF16),
        pltpu.VMEM((ROWS, INNER), BF16),
        pltpu.VMEM((ROWS, INNER), BF16),
        pltpu.VMEM((WIDTH, RANK), BF16),
        pltpu.VMEM((RANK, WIDTH), BF16),
        pltpu.VMEM((184, WIDTH), BF16),
        pltpu.VMEM((256, WIDTH), BF16),
        pltpu.VMEM((256, INNER), BF16),
        pltpu.VMEM((INNER, 128), BF16),
        pltpu.VMEM((WIDTH, 128), BF16),
        pltpu.VMEM((256, INNER), F32),
        pltpu.VMEM((544, INNER), BF16),
        pltpu.VMEM((16, 128), F32),
        dma((12,)),
    ]
    own, send, normed_t, mid, proj_part = call(
        front_kernel,
        (
            shape((2, TOK, WIDTH), BF16),
            shape((2, TOK, WIDTH), BF16),
            shape((WIDTH, ROWS), BF16),
            shape((ROWS, RANK), BF16),
            shape((WIDTH, 256), BF16),
        ),
        60,
        (flags, hidden, heads, cots, w, down, up, proj_w[0].T, expand, gather, repeat, g_row, mg, bias, decay),
        scratch,
        range(1, 11),
        (2, 4),
    )
    own, send, normed_t, mid, proj_part, hidden_got, down_a, up_a = hold(
        own, send, normed_t, mid, proj_part, hidden_got, down_a, up_a
    )
    got = swap(send, "z_lo")

    base, scale, pair_t = call(
        base_kernel,
        (shape((ROWS, WIDTH), F32), shape((ROWS, 128), F32), shape((WIDTH, ROWS), BF16)),
        8,
        (flags, hidden, hidden_got, g_row),
    )
    pair_t = pair_t.reshape(4, 4, 2, 56, ROWS)
    pair_t = jnp.concatenate([pick(pair_t, core, 2), swap(pick(pair_t, other_core, 2), "core")], -1)
    pair_t = pair_t.swapaxes(0, 1).reshape(896, 256)
    down_b, up_b = swap(down_a, "core"), swap(up_a, "core")
    pair_t, base, scale, down_a, down_b, up_a, up_b = hold(pair_t, base, scale, down_a, down_b, up_a, up_b)
    up_t, down_t = shifted(pair_t, "x", 1), shifted(pair_t, "x", 3)

    (w_both,) = call(
        wide_kernel,
        (shape((2, WIDTH, WIDTH), BF16),),
        24,
        (flags, w, down, up, down_a, down_b, up_a, up_b),
        [
            pltpu.VMEM((WIDTH, WIDTH), BF16),
            pltpu.VMEM((WIDTH, RANK), BF16),
            pltpu.VMEM((RANK, WIDTH), BF16),
            dma((7,)),
        ],
        (1,),
    )

    arriving = jnp.where(last_x, pick(final, z_lo), jnp.zeros((TOK, WIDTH), BF16))
    arriving, own, got, base, scale, w_both, down_t = hold(arriving, own, got, base, scale, w_both, down_t)
    rest = (own, got, base, scale, w_both, g_row)
    total = arriving
    for tick in range(3):
        if tick == 0:
            (previous,) = call(first_kernel, (row,), 8, (flags, arriving, *rest))
        else:
            previous, total = call(stage_kernel, (row, row), 8, (flags, arriving, total, *rest))
        arriving = lax.ppermute(previous, "x", [(3 - tick, 2 - tick)])
        if tick == 0:
            arriving, up_t = hold(arriving, up_t)
            far_t = shifted(up_t, "x", 1)
        if tick == 2:
            arriving, far_t = hold(arriving, far_t)
    own_prev, back_prev, own_act, back_act, act, shared_gain = call(
        last_kernel,
        (row, row, row, row, shape((4, ROWS, 512), BF16), shape((1, WIDTH), F32)),
        14,
        (flags, arriving, total, *rest),
    )
    got_act = swap(back_act, "z_lo")
    got_prev = swap(back_prev, "z_lo")

    act_own = lax.all_to_all(act, "x", 0, 0, tiled=True)
    act_other = swap(act_own, "core")
    lora_down, lora_up = call(
        adapter_kernel,
        (shape((WIDTH, RANK), BF16), shape((RANK, WIDTH), BF16)),
        10,
        (flags, own_act, got_act, up, normed_t, mid),
    )
    down_tiles = lora_down.reshape(4, 4, 112, 128)
    up_tiles = lora_up.reshape(16, 8, 14, 128).swapaxes(1, 2).reshape(4, 4, 112, 128)
    own_l = jnp.where(first_core, down_tiles, up_tiles)
    other_l = jnp.where(first_core, up_tiles, down_tiles)
    lora = (own_l.astype(F32) + swap(other_l, "core").astype(F32)).astype(BF16).swapaxes(0, 1)
    gain_col = shared_gain.reshape(4, 4, 2, 56)
    gain_col = (pick(gain_col, core, 2) + swap(pick(gain_col, other_core, 2), "core")).astype(BF16).swapaxes(0, 1)
    (shared,) = call(
        shared_kernel, (shape((896, 512), BF16),), 12, (flags, pair_t, up_t, far_t, down_t, act_own, act_other)
    )
    lane = lax.broadcasted_iota(jnp.int32, (4, 4, 56, 512), 3)
    tiles = lambda v, half: jnp.concatenate([v[..., :half], v[..., half:]], axis=-2)
    shared = tiles(jnp.where(lane == PART, gain_col[..., None], shared.reshape(4, 4, 56, 512)), 256)
    terms = jnp.concatenate([shared, lora], axis=-1)
    terms, proj_part = hold(terms, proj_part)
    proj_part = proj_part.reshape(4, 4, 2, 56, 256)
    proj_part = pick(proj_part, core, 2).astype(F32) + swap(pick(proj_part, other_core, 2), "core").astype(F32)
    proj_part = proj_part.astype(BF16).swapaxes(0, 1)
    terms = summed(lax.all_to_all(terms, "y", 0, 0, tiled=True), 0).astype(BF16)
    proj_sum = tiles(scattered_sum(proj_part, "y", y_places).astype(BF16), 128)
    terms = scattered_sum(jnp.concatenate([terms, proj_sum], axis=-1), "z_hi", z_places)
    proj_sum = jnp.concatenate([terms[:56, 384:], terms[56:, 384:]], axis=1)
    terms = terms.astype(BF16)

    lora = terms[:, 256:384]
    lora = jnp.stack([lora] + [shifted(lora, "z_hi", by) for by in range(1, 4)])
    block = jnp.concatenate([terms[:56, :256], terms[56:, :256]], axis=1)
    block = (block.astype(F32) + swap(block, "z_lo").astype(F32)).astype(BF16)
    lora, block = hold(lora, block)
    lora = [lora] + [shifted(lora, "y", by) for by in range(1, 4)]
    block = [block] + [shifted(block, "x", by) for by in range(1, 4)]
    lora0, lora1, lora2, lora3, *block = hold(*lora, *block)
    lora = [lora0, lora1, lora2, lora3]
    shared_grad, shared_gain_grad = call(
        columns_kernel,
        (shape((56, WIDTH), F32), shape((56, 128), F32)),
        8,
        (flags, *block),
        [pltpu.VMEM((4, 56, 512), F32)],
    )
    (lora,) = call(order_kernel, (shape((16, 112, 128), BF16),), 8, (flags, *lora))
    other = swap(lora, "core")
    down_grad = jnp.where(first_core, lora, other).reshape(WIDTH, RANK)
    up_grad = jnp.where(first_core, other, lora).reshape(16, 14, 8, 128).swapaxes(1, 2).reshape(RANK, WIDTH)
    section_grad = jnp.where(first_z, jnp.stack([own_prev, got_prev]), jnp.stack([got_prev, own_prev]))
    return (
        section_grad[None],
        shared_grad,
        shared_gain_grad[:, 0],
        down_grad[None],
        up_grad[None],
        proj_sum[None, :, :184],
        proj_sum[None, :, 184],
        proj_sum[None, :, 186],
        proj_sum[None, :, 187],
    )


def solution(mesh):
    fine = Mesh(mesh.devices.reshape(4, 4, 2, 4, 2), ("z_hi", "y", "core", "x", "z_lo"))
    return jax.shard_map(
        local,
        mesh=fine,
        in_specs=(
            P(PIPE, DP, None, None),
            P(PIPE, DP, None, None),
            P(PIPE, DP, None, None),
            P(DP, None, None),
            P(),
            P(),
            P(PIPE, None, None),
            P(PIPE, None, None),
            P(PIPE, None),
            P(PIPE, None, None),
            P(PIPE, None),
            P(PIPE, None),
        ),
        out_specs=(
            P(PIPE, DP, None, None),
            P(DP, None),
            P(DP),
            P(PIPE, None, None),
            P(PIPE, None, None),
            P(PIPE, DP, None),
            P(PIPE, DP),
            P(PIPE, None),
            P(PIPE, None),
        ),
        check_vma=False,
    )
```

```python
import jax
import jax.numpy as jnp
import numpy as np
from jax import lax
from jax.experimental import pallas as pl
from jax.experimental.pallas import tpu as pltpu
from jax.sharding import Mesh, PartitionSpec as P

EPS = 1e-05
F32 = jnp.float32
BF16 = jnp.bfloat16
HIGHEST = lax.Precision.HIGHEST

WIDTH = 1792
INNER = 3584
RANK = 128
HEADS = 56
TOK = 64
ROWS = 128
CHUNK = 256
CHUNKS = INNER // CHUNK
PART = 448

DP = ("z_hi", "y", "core")
PIPE = ("x", "z_lo")


def nn(a, b):
    return jnp.dot(a, b, preferred_element_type=F32)


def nt(a, b):
    return lax.dot_general(a, b, (((1,), (1,)), ((), ())), preferred_element_type=F32)


def exact(a, b):
    return jnp.dot(a, b, preferred_element_type=F32, precision=HIGHEST)


def two_parts(value):
    high = value.astype(BF16)
    low = (value - high.astype(F32)).astype(BF16)
    return high, low


def lanes_and_rows(shape):
    return lax.broadcasted_iota(jnp.int32, shape, 1), lax.broadcasted_iota(jnp.int32, shape, 0)


def one_hots(expand_ref, gather_ref, repeat_ref):
    lane, row = lanes_and_rows((256, CHUNK))
    for g in range(CHUNKS):
        match = ((row & (TOK - 1)) == (lane >> 6) + 4 * g) & (row < 192)
        expand_ref[:, g * CHUNK : (g + 1) * CHUNK] = jnp.where(match, 1.0, 0.0).astype(BF16)
    lane, row = lanes_and_rows((CHUNK, 128))
    for g in range(CHUNKS):
        gather_ref[g * CHUNK : (g + 1) * CHUNK] = jnp.where((row >> 6) + 4 * g == lane, 1.0, 0.0).astype(BF16)
    for g in range(WIDTH // CHUNK):
        place = row + g * CHUNK
        quotient = (place * 18725) >> 20
        repeat_ref[g * CHUNK : (g + 1) * CHUNK] = jnp.where(place - 56 * quotient == lane, 1.0, 0.0).astype(BF16)


def ssd_back(bc, raw, decay_row, expand, gather, head_ref, cot_ref, expanded, stack):
    lane128, _ = lanes_and_rows((TOK, 128))
    low_half = lane128 < TOK
    lane64, row64 = lanes_and_rows((TOK, TOK))
    lower = (row64 >= lane64).astype(F32)
    upper = (row64 <= lane64).astype(F32)
    steps, parts = [], []
    for n in range(2):
        step = jax.nn.softplus(raw[n * TOK : (n + 1) * TOK])
        step = jnp.where(lane128 < HEADS, step, 0.0)
        running = exact(lower, step)
        steps.append(step)
        for value in (running, step):
            first = value.astype(BF16).astype(F32)
            rest = value - first
            second = rest.astype(BF16).astype(F32)
            third = rest - second
            left = jnp.where(low_half, first, pltpu.roll(second, TOK, 1))
            parts.append(jnp.concatenate([left, third], axis=1).astype(BF16))
    expanded[...] = nn(jnp.concatenate(parts, axis=0), expand[...])
    decay_wide = jnp.broadcast_to(decay_row, (8, 128))
    d_first = decay_wide.astype(BF16).astype(F32)
    d_rest = decay_wide - d_first
    d_second = d_rest.astype(BF16).astype(F32)
    lane8, _ = lanes_and_rows((8, 128))
    d_left = jnp.where(lane8 < TOK, d_first, pltpu.roll(d_second, TOK, 1))
    d_parts = jnp.concatenate([d_left, d_rest - d_second], axis=1).astype(BF16)
    decay_lanes = nn(d_parts, expand[...])[0:1]

    lane_c, row_c = lanes_and_rows((TOK, CHUNK))
    token_c = lane_c % TOK
    causal = row_c >= token_c
    diagonal = row_c == token_c
    lane_b, row_b = lanes_and_rows((CHUNK, CHUNK))
    block = (lane_b // TOK) == (row_b // TOK)
    row16 = lax.broadcasted_iota(jnp.int32, (16, CHUNK), 0)
    d_bc = []
    for n in range(2):
        rows = slice(n * TOK, (n + 1) * TOK)
        here = bc[rows]
        rolled = pltpu.roll(here, TOK, 1)
        b_only = jnp.where(low_half, here, 0.0)
        crossing = lax.dot_general(
            rolled,
            jnp.concatenate([b_only] * 4, axis=0),
            (((1,), (1,)), ((), ())),
            preferred_element_type=F32,
            precision=HIGHEST,
        )
        d_cross = jnp.zeros((TOK, CHUNK), F32)
        for g in range(CHUNKS):
            cols = slice(g * CHUNK, (g + 1) * CHUNK)
            heads = jnp.concatenate([head_ref[rows, cols]] * 4, axis=0)
            heads = jnp.where(block, heads, jnp.zeros_like(heads))
            grad = nt(cot_ref[rows, cols], heads)
            run = expanded[n * ROWS : n * ROWS + TOK, cols]
            step = expanded[n * ROWS + TOK : (n + 1) * ROWS, cols]
            run_j = jnp.sum(jnp.where(diagonal, run, 0.0), axis=0, keepdims=True)
            step_j = jnp.sum(jnp.where(diagonal, step, 0.0), axis=0, keepdims=True)
            spread = jnp.where(causal, run - run_j, 0.0)
            kernel = jnp.where(causal, jnp.exp(-decay_lanes[:, cols] * spread), 0.0)
            scored = grad * kernel
            d_cross = d_cross + scored * step_j
            per_step = scored * crossing
            col = jnp.sum(per_step, axis=0, keepdims=True)
            mass = per_step * step_j
            balance = mass - jnp.where(diagonal, col * step_j, 0.0)
            direct = jnp.where(diagonal, col, 0.0)
            spent = jnp.sum(mass * spread, axis=0, keepdims=True)
            base_row = n * 272
            high, low = two_parts(balance)
            stack[base_row : base_row + 64, cols] = high
            stack[base_row + 64 : base_row + 128, cols] = low
            high, low = two_parts(direct)
            stack[base_row + 128 : base_row + 192, cols] = high
            stack[base_row + 192 : base_row + 256, cols] = low
            high = spent.astype(BF16).astype(F32)
            tail = jnp.where(row16 == 0, high, jnp.where(row16 == 1, spent - high, 0.0))
            stack[base_row + 256 : base_row + 272, cols] = tail.astype(BF16)
        d_cross = d_cross[:, :128] + d_cross[:, 128:]
        d_cross = (d_cross + pltpu.roll(d_cross, TOK, 1))[:, :TOK]
        c_low = jnp.where(low_half, rolled, 0.0)
        b_high = jnp.where(low_half, 0.0, rolled)
        d_bc.append(exact(d_cross.T, c_low) + exact(d_cross, b_high))
    gathered = nn(stack[...], gather[...])
    d_raw, decay_cot = [], jnp.zeros((1, 128), F32)
    for n in range(2):
        at = n * 272
        balance = gathered[at : at + 64] + gathered[at + 64 : at + 128]
        direct = gathered[at + 128 : at + 192] + gathered[at + 192 : at + 256]
        spent = jnp.sum(gathered[at + 256 : at + 272], axis=0, keepdims=True)
        d_step = direct + exact(upper, -decay_row * balance)
        d_raw.append(d_step * jax.nn.sigmoid(raw[n * TOK : (n + 1) * TOK]))
        decay_cot = decay_cot - spent
    return jnp.concatenate(d_bc, axis=0), jnp.concatenate(d_raw, axis=0), decay_cot


def front_kernel(
    flags_ref, hidden_any, head_any, cot_any, w_any, down_any, up_any, proj_any,
    g_ref, mg_ref, bias_ref, decay_ref,
    own_ref, send_ref, normed_t_any, mid_ref, proj_out_any,
    normed_t_ref, proj_ref, w_ref, hidden_ref, head_ref, cot_ref, down_ref, up_ref, proj_near, proj_w, expand_ref, gather_ref, repeat_ref, expanded, stack, padded, sems,
):
    copies = []
    pairs = (
        (hidden_any, hidden_ref),
        (down_any, down_ref),
        (w_any, w_ref),
        (up_any, up_ref),
        (proj_any, proj_near),
        (head_any, head_ref),
        (cot_any, cot_ref),
    )
    for k, (source, target) in enumerate(pairs):
        copies.append(pltpu.make_async_copy(source, target, sems.at[k]))
        copies[-1].start()
    one_hots(expand_ref, gather_ref, repeat_ref)
    padded[...] = jnp.zeros_like(padded)
    padded[0:1, 0:HEADS] = bias_ref[...]
    padded[8:9, 0:HEADS] = decay_ref[...]
    copies[0].wait()
    stream = hidden_ref[...].astype(F32)
    scale0 = lax.rsqrt(jnp.mean(stream * stream, axis=1, keepdims=True) + EPS)
    normed = (stream * scale0 * g_ref[...]).astype(BF16)
    normed_t_ref[...] = normed.T
    copies.append(pltpu.make_async_copy(normed_t_ref, normed_t_any, sems.at[7]))
    copies[7].start()
    copies[1].wait()
    mid = nn(normed, down_ref[...]).astype(BF16)
    mid_ref[...] = mid
    copies[2].wait()
    copies[3].wait()
    act = nn(normed, w_ref[...]) + nn(mid, up_ref[...])
    gate = jax.nn.sigmoid(act)
    slope = gate * (1.0 + act * (1.0 - gate))
    middle = stream + act * gate
    scale1 = lax.rsqrt(jnp.mean(middle * middle, axis=1, keepdims=True) + EPS)
    inner = middle * scale1
    gain = mg_ref[...]
    mamba_in = (inner * gain).astype(BF16)
    for k in range(4, 7):
        copies[k].wait()
    proj_w[...] = jnp.zeros_like(proj_w)
    proj_w[0:184] = proj_near[...]
    bc = nt(mamba_in, proj_w[0:128])
    raw = nt(mamba_in, proj_w[128:256]) + padded[0:1]
    d_bc, d_raw, decay_cot = ssd_back(
        bc, raw, padded[8:9], expand_ref, gather_ref, head_ref, cot_ref, expanded, stack
    )
    d_proj = jnp.concatenate([d_bc.astype(BF16), d_raw.astype(BF16)], axis=1)
    mamba_cot = nn(d_proj, proj_w[...])
    pulled = mamba_cot * inner
    weighted = mamba_cot * gain
    const = scale1 * (weighted - inner * jnp.mean(pulled * gain, axis=1, keepdims=True))
    second = flags_ref[0] == 1
    for k, value in enumerate((const, slope)):
        low, high = value[:TOK].astype(BF16), value[TOK:].astype(BF16)
        own_ref[k] = jnp.where(second, high, low)
        send_ref[k] = jnp.where(second, low, high)
    lane, row = lanes_and_rows((ROWS, 256))
    ones = jnp.where(lane == 184, 1.0, 0.0).astype(BF16)
    small = jnp.concatenate(
        [jnp.sum(d_raw, axis=0, keepdims=True), decay_cot, jnp.zeros((6, 128), F32)], axis=0
    ).T
    small = jnp.where(lane == 186, small[:, 0:1], jnp.where(lane == 187, small[:, 1:2], 0.0)).astype(BF16)
    proj_ref[...] = (
        nn(mamba_in.T, d_proj) + nn(pulled.astype(BF16).T, ones) + nn(repeat_ref[...], small)
    ).astype(BF16)
    out = pltpu.make_async_copy(proj_ref, proj_out_any, sems.at[8])
    out.start()
    copies[7].wait()
    out.wait()


def slice_kernel(
    flags_ref, hidden_any, down_any, up_any, hidden_out, down_out, up_out, hidden_near, down_near, up_near, sems
):
    here, core = flags_ref[0], flags_ref[1]
    half = WIDTH // 2
    steps = (
        (hidden_any.at[pl.ds(pl.multiple_of((1 - here) * TOK, TOK), TOK)], hidden_near, hidden_out),
        (down_any.at[pl.ds(pl.multiple_of(core * half, half), half)], down_near, down_out),
        (up_any.at[pl.ds(pl.multiple_of(core * 64, 64), 64)], up_near, up_out),
    )
    first = [pltpu.make_async_copy(source, near, sems.at[k]) for k, (source, near, _) in enumerate(steps)]
    second = [pltpu.make_async_copy(near, target, sems.at[3 + k]) for k, (_, near, target) in enumerate(steps)]
    for copy in first:
        copy.start()
    for one, two in zip(first, second):
        one.wait()
        two.start()
    for copy in second:
        copy.wait()


def base_kernel(flags_ref, hidden_ref, hidden_got_ref, g_ref, base_ref, scale_ref, normed_t_ref):
    here = flags_ref[0]
    later = here == 1
    own = hidden_ref[pl.ds(pl.multiple_of(here * TOK, TOK), TOK), :].astype(F32)
    got = hidden_got_ref[...].astype(F32)
    stream = jnp.concatenate([jnp.where(later, own, got), jnp.where(later, got, own)], axis=0)
    scale0 = lax.rsqrt(jnp.mean(stream * stream, axis=1, keepdims=True) + EPS)
    base = stream * scale0
    base_ref[...] = base
    scale_ref[...] = jnp.broadcast_to(scale0, (ROWS, 128))
    normed_t_ref[...] = (base * g_ref[...]).astype(BF16).T


def wide_kernel(
    flags_ref, w_any, down_ref, up_ref, down_a_ref, down_b_ref, up_a_ref, up_b_ref, wide_ref,
    w_ref, down_got, up_got, own_down_t, got_down_t, sems,
):
    copies = []
    for n in range(WIDTH // 256):
        rows = pl.ds(n * 256, 256)
        copies.append(pltpu.make_async_copy(w_any.at[rows], w_ref.at[rows], sems.at[n]))
        copies[-1].start()
    here, core = flags_ref[0], flags_ref[1]
    half = WIDTH // 2
    down_got[pl.ds(pl.multiple_of(core * half, half), half), :] = down_a_ref[...]
    down_got[pl.ds(pl.multiple_of((1 - core) * half, half), half), :] = down_b_ref[...]
    up_got[pl.ds(pl.multiple_of(core * 64, 64), 64), :] = up_a_ref[...]
    up_got[pl.ds(pl.multiple_of((1 - core) * 64, 64), 64), :] = up_b_ref[...]
    mine, other = 1 - here, here
    own_up, got_up = up_ref[...].T, up_got[...].T
    own_down, got_down = down_ref[...].T, down_got[...].T
    own_down_t[...], got_down_t[...] = own_down, got_down

    def block(n, _):
        cols = pl.ds(pl.multiple_of(n * CHUNK, CHUNK), CHUNK)
        part = w_ref[cols, :].T.astype(F32)
        wide_ref[mine, :, cols] = (part + nn(own_up, own_down_t[:, cols])).astype(BF16)
        wide_ref[other, :, cols] = (part + nn(got_up, got_down_t[:, cols])).astype(BF16)
        return 0

    for copy in copies:
        copy.wait()
    lax.fori_loop(0, WIDTH // CHUNK, block, 0)


def section_math(k, arriving, later, own_ref, got_ref, base_ref, scale_ref, wide_ref, g_ref):
    rows = slice(k * TOK, (k + 1) * TOK)
    use_own = later if k == 0 else jnp.logical_not(later)
    const = jnp.where(use_own, own_ref[0], got_ref[0]).astype(F32)
    slope = jnp.where(use_own, own_ref[1], got_ref[1]).astype(F32)
    base = base_ref[rows]
    stream_cot = arriving + const
    act_cot = (stream_cot * slope).astype(BF16)
    normed_cot = nn(act_cot, wide_ref[k])
    pulled = normed_cot * g_ref[...]
    previous = stream_cot + scale_ref[rows, 0:1] * (
        pulled - base * jnp.mean(pulled * base, axis=1, keepdims=True)
    )
    return previous.astype(BF16), act_cot, normed_cot * base


def first_kernel(flags_ref, arriving_ref, *refs):
    previous_ref = refs[-1]
    later = flags_ref[0] == 1
    value = arriving_ref[...]
    for k in range(2):
        value = section_math(k, value.astype(F32), later, *refs[:-1])[0]
    previous_ref[...] = value


def stage_kernel(flags_ref, arriving_ref, total_ref, *refs):
    previous_ref, sum_ref = refs[-2:]
    later = flags_ref[0] == 1
    value = arriving_ref[...]
    sum_ref[...] = (total_ref[...].astype(F32) + value.astype(F32)).astype(BF16)
    for k in range(2):
        value = section_math(k, value.astype(F32), later, *refs[:-2])[0]
    previous_ref[...] = value


def last_kernel(flags_ref, arriving_ref, total_ref, *refs):
    own_prev_ref, back_prev_ref, own_act_ref, back_act_ref, act_ref, shared_gain_ref = refs[-6:]
    later = flags_ref[0] == 1
    value = (arriving_ref[...].astype(F32) + total_ref[...].astype(F32)).astype(BF16)
    previous, acts, gains = [], [], jnp.zeros((1, WIDTH), F32)
    for k in range(2):
        value, act_cot, product = section_math(k, value.astype(F32), later, *refs[:-6])
        previous.append(value)
        acts.append(act_cot)
        gains = gains + jnp.sum(product, axis=0, keepdims=True)
    for pair, own_out, back_out in ((previous, own_prev_ref, back_prev_ref), (acts, own_act_ref, back_act_ref)):
        own_out[...] = jnp.where(later, pair[0], pair[1])
        back_out[...] = jnp.where(later, pair[1], pair[0])
    padded = jnp.concatenate([jnp.concatenate(acts, axis=0), jnp.zeros((ROWS, 128), BF16)], axis=1)
    for q in range(4):
        act_ref[q] = padded[:, q * PART : q * PART + 512]
    shared_gain_ref[...] = gains


def adapter_kernel(flags_ref, own_ref, got_ref, up_ref, normed_t_ref, mid_ref, down_grad_ref, up_grad_ref):
    first = flags_ref[0] == 0
    own, got = own_ref[...], got_ref[...]
    act_cot = jnp.concatenate([jnp.where(first, own, got), jnp.where(first, got, own)], axis=0)
    mid_cot = nt(act_cot, up_ref[...]).astype(BF16)
    down_grad_ref[...] = nn(normed_t_ref[...], mid_cot).astype(BF16)
    up_grad_ref[...] = nn(mid_ref[...].T, act_cot).astype(BF16)


def shared_kernel(flags_ref, t0_ref, t1_ref, t2_ref, t3_ref, act_own_ref, act_other_ref, out_ref):
    x = flags_ref[2]
    total = jnp.zeros((WIDTH // 2, 512), F32)
    for back, ref in enumerate((t0_ref, t1_ref, t2_ref, t3_ref)):
        source = jnp.where(x >= back, x - back, x - back + 4)
        right = jnp.concatenate([act_own_ref[source], act_other_ref[source]], axis=0)
        total = total + nn(ref[...], right)
    out_ref[...] = total.astype(BF16)


def order_kernel(flags_ref, *refs):
    y, z_hi = flags_ref[3], flags_ref[4]
    out_ref = refs[-1]
    for by, ref in enumerate(refs[:-1]):
        row = jnp.where(y >= by, y - by, y - by + 4)
        for bz in range(4):
            out_ref[jnp.where(z_hi >= bz, z_hi - bz, z_hi - bz + 4) * 4 + row] = ref[bz]


def columns_kernel(flags_ref, *refs):
    x = flags_ref[2]
    shared_ref, gain_ref, blocks = refs[-3:]
    for back, ref in enumerate(refs[:-3]):
        blocks[jnp.where(x >= back, x - back, x - back + 4)] = ref[...].astype(F32)
    parts, gain = [], jnp.zeros((56, 1), F32)
    for q in range(4):
        block = blocks[q]
        parts.append(block[:, :PART])
        gain = gain + block[:, PART : PART + 1]
    shared_ref[...] = jnp.concatenate(parts, axis=1)
    gain_ref[...] = jnp.broadcast_to(gain, (56, 128))


def shape(dims, dtype):
    return jax.ShapeDtypeStruct(dims, dtype)


def call(kernel, outs, megabytes, args, scratch=(), copied=(), out_copied=()):
    place = lambda k, chosen: pl.BlockSpec(memory_space=pltpu.HBM) if k in chosen else pl.BlockSpec()
    return pl.pallas_call(
        kernel,
        out_shape=tuple(outs),
        in_specs=[pl.BlockSpec(memory_space=pltpu.SMEM)] + [place(k, copied) for k in range(1, len(args))],
        out_specs=tuple(place(k, out_copied) for k in range(len(outs))),
        scratch_shapes=list(scratch),
        compiler_params=pltpu.CompilerParams(vmem_limit_bytes=megabytes * 1024 * 1024),
        cost_estimate=pl.CostEstimate(flops=1_000, bytes_accessed=1_000, transcendentals=0),
    )(*args)


def swap(value, axis):
    return lax.ppermute(value, axis, [(0, 1), (1, 0)])


def pick(value, index, axis=0):
    return lax.dynamic_index_in_dim(value, index, axis, keepdims=False, allow_negative_indices=False)


def shifted(value, axis, by):
    return lax.ppermute(value, axis, [(i, (i + by) % 4) for i in range(4)])


def scattered_sum(value, axis, places):
    total = pick(value, places[0]).astype(F32)
    for by in range(1, 4):
        total = total + shifted(pick(value, places[by]), axis, by).astype(F32)
    return total


def summed(value, axis):
    return jnp.sum(value.astype(F32), axis=axis)


def hold(*values):
    return lax.optimization_barrier(values)


def local(hidden, heads, cots, final, w, g, down, up, mg, proj_w, bias, decay):
    core, x, z_lo = lax.axis_index("core"), lax.axis_index("x"), lax.axis_index("z_lo")
    y, z_hi = lax.axis_index("y"), lax.axis_index("z_hi")
    flags = jnp.stack([z_lo, core, x, y, z_hi]).astype(jnp.int32)
    y_places = [y] + [jnp.where(y + by < 4, y + by, y + by - 4) for by in range(1, 4)]
    z_places = [z_hi] + [jnp.where(z_hi + by < 4, z_hi + by, z_hi + by - 4) for by in range(1, 4)]
    first_core, first_z, last_x = core == 0, z_lo == 0, x == 3
    down, up = down[0], up[0]
    hidden, heads, cots = (a[0].reshape(ROWS, a.shape[-1]) for a in (hidden, heads, cots))
    flags, y_places, z_places, core, other_core, z_lo, first_core, first_z, last_x, hidden = lax.optimization_barrier(
        (flags, y_places, z_places, core, 1 - core, z_lo, first_core, first_z, last_x, hidden)
    )
    g_row = g[None]
    row = shape((TOK, WIDTH), BF16)
    dma = pltpu.SemaphoreType.DMA

    hidden_send, down_send, up_send = call(
        slice_kernel,
        (row, shape((WIDTH // 2, RANK), BF16), shape((64, WIDTH), BF16)),
        60,
        (flags, hidden, down, up),
        [
            pltpu.VMEM((TOK, WIDTH), BF16),
            pltpu.VMEM((WIDTH // 2, RANK), BF16),
            pltpu.VMEM((64, WIDTH), BF16),
            dma((6,)),
        ],
        (1, 2, 3),
        (0, 1, 2),
    )
    hidden_got = swap(hidden_send, "z_lo")
    down_a, up_a = swap(down_send, "z_lo"), swap(up_send, "z_lo")

    scratch = [
        pltpu.VMEM((WIDTH, ROWS), BF16),
        pltpu.VMEM((WIDTH, 256), BF16),
        pltpu.VMEM((WIDTH, WIDTH), BF16),
        pltpu.VMEM((ROWS, WIDTH), BF16),
        pltpu.VMEM((ROWS, INNER), BF16),
        pltpu.VMEM((ROWS, INNER), BF16),
        pltpu.VMEM((WIDTH, RANK), BF16),
        pltpu.VMEM((RANK, WIDTH), BF16),
        pltpu.VMEM((184, WIDTH), BF16),
        pltpu.VMEM((256, WIDTH), BF16),
        pltpu.VMEM((256, INNER), BF16),
        pltpu.VMEM((INNER, 128), BF16),
        pltpu.VMEM((WIDTH, 128), BF16),
        pltpu.VMEM((256, INNER), F32),
        pltpu.VMEM((544, INNER), BF16),
        pltpu.VMEM((16, 128), F32),
        dma((9,)),
    ]
    own, send, normed_t, mid, proj_part = call(
        front_kernel,
        (
            shape((2, TOK, WIDTH), BF16),
            shape((2, TOK, WIDTH), BF16),
            shape((WIDTH, ROWS), BF16),
            shape((ROWS, RANK), BF16),
            shape((WIDTH, 256), BF16),
        ),
        60,
        (flags, hidden, heads, cots, w, down, up, proj_w[0].T, g_row, mg, bias, decay),
        scratch,
        range(1, 8),
        (2, 4),
    )
    own, send, normed_t, mid, proj_part, hidden_got, down_a, up_a = hold(
        own, send, normed_t, mid, proj_part, hidden_got, down_a, up_a
    )
    got = swap(send, "z_lo")

    base, scale, pair_t = call(
        base_kernel,
        (shape((ROWS, WIDTH), F32), shape((ROWS, 128), F32), shape((WIDTH, ROWS), BF16)),
        8,
        (flags, hidden, hidden_got, g_row),
    )
    pair_t = pair_t.reshape(4, 4, 2, 56, ROWS)
    pair_t = jnp.concatenate([pick(pair_t, core, 2), swap(pick(pair_t, other_core, 2), "core")], -1)
    pair_t = pair_t.swapaxes(0, 1).reshape(896, 256)
    down_b, up_b = swap(down_a, "core"), swap(up_a, "core")
    pair_t, base, scale, down_a, down_b, up_a, up_b = hold(pair_t, base, scale, down_a, down_b, up_a, up_b)
    up_t, down_t = shifted(pair_t, "x", 1), shifted(pair_t, "x", 3)

    (w_both,) = call(
        wide_kernel,
        (shape((2, WIDTH, WIDTH), BF16),),
        24,
        (flags, w, down, up, down_a, down_b, up_a, up_b),
        [
            pltpu.VMEM((WIDTH, WIDTH), BF16),
            pltpu.VMEM((WIDTH, RANK), BF16),
            pltpu.VMEM((RANK, WIDTH), BF16),
            pltpu.VMEM((RANK, WIDTH), BF16),
            pltpu.VMEM((RANK, WIDTH), BF16),
            dma((7,)),
        ],
        (1,),
    )

    arriving = jnp.where(last_x, pick(final, z_lo), jnp.zeros((TOK, WIDTH), BF16))
    arriving, own, got, base, scale, w_both, down_t = hold(arriving, own, got, base, scale, w_both, down_t)
    rest = (own, got, base, scale, w_both, g_row)
    total = arriving
    for tick in range(3):
        if tick == 0:
            (previous,) = call(first_kernel, (row,), 8, (flags, arriving, *rest))
        else:
            previous, total = call(stage_kernel, (row, row), 8, (flags, arriving, total, *rest))
        arriving = lax.ppermute(previous, "x", [(3 - tick, 2 - tick)])
        if tick == 0:
            arriving, up_t = hold(arriving, up_t)
            far_t = shifted(up_t, "x", 1)
        if tick == 2:
            arriving, far_t = hold(arriving, far_t)
    own_prev, back_prev, own_act, back_act, act, shared_gain = call(
        last_kernel,
        (row, row, row, row, shape((4, ROWS, 512), BF16), shape((1, WIDTH), F32)),
        14,
        (flags, arriving, total, *rest),
    )
    got_act = swap(back_act, "z_lo")
    got_prev = swap(back_prev, "z_lo")

    act_own = lax.all_to_all(act, "x", 0, 0, tiled=True)
    act_other = swap(act_own, "core")
    lora_down, lora_up = call(
        adapter_kernel,
        (shape((WIDTH, RANK), BF16), shape((RANK, WIDTH), BF16)),
        10,
        (flags, own_act, got_act, up, normed_t, mid),
    )
    down_tiles = lora_down.reshape(4, 4, 112, 128)
    up_tiles = lora_up.reshape(16, 8, 14, 128).swapaxes(1, 2).reshape(4, 4, 112, 128)
    own_l = jnp.where(first_core, down_tiles, up_tiles)
    other_l = jnp.where(first_core, up_tiles, down_tiles)
    lora = (own_l.astype(F32) + swap(other_l, "core").astype(F32)).astype(BF16).swapaxes(0, 1)
    gain_col = shared_gain.reshape(4, 4, 2, 56)
    gain_col = (pick(gain_col, core, 2) + swap(pick(gain_col, other_core, 2), "core")).astype(BF16).swapaxes(0, 1)
    (shared,) = call(
        shared_kernel, (shape((896, 512), BF16),), 12, (flags, pair_t, up_t, far_t, down_t, act_own, act_other)
    )
    lane = lax.broadcasted_iota(jnp.int32, (4, 4, 56, 512), 3)
    tiles = lambda v, half: jnp.concatenate([v[..., :half], v[..., half:]], axis=-2)
    shared = tiles(jnp.where(lane == PART, gain_col[..., None], shared.reshape(4, 4, 56, 512)), 256)
    terms = jnp.concatenate([shared, lora], axis=-1)
    terms, proj_part = hold(terms, proj_part)
    proj_part = proj_part.reshape(4, 4, 2, 56, 256)
    proj_part = pick(proj_part, core, 2).astype(F32) + swap(pick(proj_part, other_core, 2), "core").astype(F32)
    proj_part = proj_part.astype(BF16).swapaxes(0, 1)
    terms = summed(lax.all_to_all(terms, "y", 0, 0, tiled=True), 0).astype(BF16)
    proj_sum = tiles(scattered_sum(proj_part, "y", y_places).astype(BF16), 128)
    terms = scattered_sum(jnp.concatenate([terms, proj_sum], axis=-1), "z_hi", z_places)
    proj_sum = jnp.concatenate([terms[:56, 384:], terms[56:, 384:]], axis=1)
    terms = terms.astype(BF16)

    lora = terms[:, 256:384]
    lora = jnp.stack([lora] + [shifted(lora, "z_hi", by) for by in range(1, 4)])
    block = jnp.concatenate([terms[:56, :256], terms[56:, :256]], axis=1)
    block = (block.astype(F32) + swap(block, "z_lo").astype(F32)).astype(BF16)
    lora, block = hold(lora, block)
    lora = [lora] + [shifted(lora, "y", by) for by in range(1, 4)]
    block = [block] + [shifted(block, "x", by) for by in range(1, 4)]
    lora0, lora1, lora2, lora3, *block = hold(*lora, *block)
    lora = [lora0, lora1, lora2, lora3]
    shared_grad, shared_gain_grad = call(
        columns_kernel,
        (shape((56, WIDTH), F32), shape((56, 128), F32)),
        8,
        (flags, *block),
        [pltpu.VMEM((4, 56, 512), F32)],
    )
    (lora,) = call(order_kernel, (shape((16, 112, 128), BF16),), 8, (flags, *lora))
    other = swap(lora, "core")
    down_grad = jnp.where(first_core, lora, other).reshape(WIDTH, RANK)
    up_grad = jnp.where(first_core, other, lora).reshape(16, 14, 8, 128).swapaxes(1, 2).reshape(RANK, WIDTH)
    section_grad = jnp.where(first_z, jnp.stack([own_prev, got_prev]), jnp.stack([got_prev, own_prev]))
    return (
        section_grad[None],
        shared_grad,
        shared_gain_grad[:, 0],
        down_grad[None],
        up_grad[None],
        proj_sum[None, :, :184],
        proj_sum[None, :, 184],
        proj_sum[None, :, 186],
        proj_sum[None, :, 187],
    )


def solution(mesh):
    fine = Mesh(mesh.devices.reshape(4, 4, 2, 4, 2), ("z_hi", "y", "core", "x", "z_lo"))
    return jax.shard_map(
        local,
        mesh=fine,
        in_specs=(
            P(PIPE, DP, None, None),
            P(PIPE, DP, None, None),
            P(PIPE, DP, None, None),
            P(DP, None, None),
            P(),
            P(),
            P(PIPE, None, None),
            P(PIPE, None, None),
            P(PIPE, None),
            P(PIPE, None, None),
            P(PIPE, None),
            P(PIPE, None),
        ),
        out_specs=(
            P(PIPE, DP, None, None),
            P(DP, None),
            P(DP),
            P(PIPE, None, None),
            P(PIPE, None, None),
            P(PIPE, DP, None),
            P(PIPE, DP),
            P(PIPE, None),
            P(PIPE, None),
        ),
        check_vma=False,
    )
```
